128 devices in a mesh: lat: 8 (over z, x_hi), lon: 16 (over y, x_lo, core).
Axes of the slice: x: 4 (x_hi: 2, x_lo: 2; x = x_hi * 2 + x_lo), y: 4, z: 4, core: 2. Of those that a mesh axis runs over, the one named last changes fastest.
Arguments:
- w_obs: float32 [2, 524288], P(None, ('lat', 'lon')), may hold values from -6 to 6
- r_obs: float32 [2, 524288], P(None, ('lat', 'lon')), may hold values from -16 to 16
- p_obs: float32 [2, 524288], P(None, ('lat', 'lon')), may hold values from -16 to 16
- obs_dest: int32 [524288, 1], P(('lat', 'lon')), may hold values from 0 to 127; in each aligned block of 4096 rows (0 to 4095, 4096 to 8191, ...) at most 64 rows name the same one
- obs_row: int32 [524288], P(('lat', 'lon')), may hold values from 0 to 62
- obs_col: int32 [524288], P(('lat', 'lon')), may hold values from 0 to 126
- obs_level: int32 [524288], P(('lat', 'lon')), may hold values from 0 to 7
- obs_field: int32 [524288], P(('lat', 'lon')), may hold values from 0 to 3
- obs_frac: float32 [2, 524288], P(None, ('lat', 'lon')), may hold values from 0 to 1
- obs_var: float32 [524288], P(('lat', 'lon')), may hold values from 0.5 to 2
- corr_panel: bfloat16 [16, 512, 512], P('lon', None, 'lat'), may hold values from -1 to 1, as said below
- sigma_b: float32 [4, 8, 512, 2048], P(None, None, 'lat', 'lon'), may hold values from 0.5 to 2
- coef_lat: float32 [4, 8, 512, 2048], P(None, None, 'lat', 'lon'), may hold values from 0.02 to 0.24
- coef_lon: float32 [4, 8, 512, 2048], P(None, None, 'lat', 'lon'), may hold values from 0.02 to 0.24
Outputs:
- w_next: float32 [2, 524288], P(None, ('lat', 'lon'))
- r_next: float32 [2, 524288], P(None, ('lat', 'lon'))
- p_next: float32 [2, 524288], P(None, ('lat', 'lon'))
The draws below stay inside these ranges and needn't reach their ends.
Inputs may be any that keep to these rules, and one draw needn't show every extreme that they name: `obs_dest`: numbers devices in the order lat then lon; in the rows of one device no device is named by more than 64 rows, and some device is named by exactly 64. `corr_panel`: symmetric in its last two dimensions with ones on the diagonal.
All inputs are finite; a program needn't handle non-finite values.
Results may differ from the reference program's by a relative error of at most 0.0018.
Values may be sent and summed in bfloat16 or wider, within the bound.
No kernel may reach another device: no remote copies, remote signals or barrier semaphores. Data moves between devices by JAX's collectives and lax.ppermute only.
A program may use at most 128 MiB of HBM per device.

```python
import math
import jax
import jax.numpy as jnp
import numpy as np
from jax import lax

M = 2
F = 4
LEV = 8
CLAT = 64
CLON = 128
OBS_DEV = 4096
RC = 64
DSTEPS = 4
LAT = 512
LON = 2048
NOBS = 524288
CAP = 64
NCORR = 512
N_LAT = 8
N_LON = 16
DEVICES = 128


def obs_vector(key):
    device_ids = jnp.arange(NOBS, dtype=jnp.int32) // OBS_DEV
    device_total = NOBS // OBS_DEV
    rising = 1.0 + 2.0 * device_ids.astype(jnp.float32) / max(device_total - 1, 1)
    values = jnp.clip(jax.random.normal(key, (M, NOBS), jnp.float32), -5.0, 5.0)
    return values * rising[None, :]


def draw_r_obs(key, part):
    return obs_vector(jax.random.fold_in(key, 11))


def draw_p_obs(key, part):
    return obs_vector(jax.random.fold_in(key, 23))


def draw_corr_panel(key, part):
    inner_key = jax.random.fold_in(key, 37)
    spread_scale = 0.35 / NCORR ** 0.5
    raw = jnp.clip(jax.random.normal(inner_key, (N_LON, NCORR, NCORR), jnp.float32), -4.0, 4.0) * spread_scale
    symmetric = 0.5 * (raw + jnp.swapaxes(raw, 1, 2))
    diagonal = (jnp.arange(NCORR)[:, None] == jnp.arange(NCORR)[None, :]).astype(jnp.float32)
    return (symmetric * (1.0 - diagonal)[None] + diagonal[None]).astype(jnp.bfloat16)


def touch_ends(array, own_key, smallest, high):
    extent = array.shape
    place = [jax.random.randint(jax.random.fold_in(own_key, axis), (), 0, extent[axis]) for axis in range(len(extent))]
    array = array.at[tuple(place)].set(smallest)
    longest = extent.index(max(extent))
    place[longest] = (place[longest] + 1) % extent[longest]
    return array.at[tuple(place)].set(high)


def steps_of(own_key, shape, cuts, least, top_value):
    def one(axis_at, parts):
        draws = jax.random.uniform(jax.random.fold_in(jax.random.fold_in(own_key, 6), axis_at), (parts,), jnp.float32, least / len(cuts), top_value / len(cuts))
        return jnp.repeat(jnp.exp(draws), shape[axis_at] // parts).reshape((-1,) + (1,) * (len(shape) - axis_at - 1))

    gain = one(*cuts[0])
    for cut in cuts[1:]:
        gain = gain * one(*cut)
    return gain


def assign_block(key, own, number, rows, count, top, most, skew):
    sequence = jax.random.permutation(key, count)
    packed, usual = shares(count, rows * top, most, skew, True), shares(count, rows * top, most, skew, False)
    places = jnp.arange(count)

    def named(lengths, turn):
        used = int((lengths > 0).sum())
        fixed = max(1, used // 4)
        shifted = fixed + (places - fixed + turn * (used - fixed)) % max(1, count - fixed)
        return jnp.zeros((count,), jnp.int32).at[sequence[jnp.where(places < fixed, places, shifted)]].set(jnp.asarray(lengths, jnp.int32))

    lengths = jnp.where(number % 4 == 0, named(packed, number // 4), named(usual, number - number // 4 - 1))
    mixed = jax.random.permutation(jax.random.fold_in(own, 3), count)
    source_of, sink = mixed[0:count // 2 * 2:2], mixed[1:count // 2 * 2:2]
    slack = jnp.minimum(lengths[source_of] - 1, most - lengths[sink]) // 2
    slack = jnp.where((source_of == sequence[0]) | (sink == sequence[0]) | (lengths[sink] == 0), 0, jnp.maximum(slack, 0))
    shifted = jax.random.randint(jax.random.fold_in(own, 4), (count // 2,), 0, 1 << 20) % (slack + 1)
    lengths = lengths.at[source_of].add(-shifted).at[sink].add(shifted)
    items = jnp.searchsorted(jnp.cumsum(lengths), jnp.arange(rows * top), side="right").astype(jnp.int32)
    table = items.reshape(top, rows).T
    table = table[jax.random.permutation(jax.random.fold_in(own, 1), rows)]
    turn = jax.random.randint(jax.random.fold_in(own, 2), (rows, 1), 0, top)
    return jnp.take_along_axis(table, (jnp.arange(top)[None, :] + turn) % top, axis=1)


def shares(number_of, total, limit, lean, full):
    loads = [(1 << 20) // math.isqrt(rank ** lean) + 1 for rank in range(1, number_of + 1)]
    largest = limit if full else min(limit, max(-(-total // number_of), total * loads[0] // sum(loads)))
    least = 1 if total - largest >= number_of - 1 else 0
    counts, surplus = [largest] + [least] * (number_of - 1), total - largest - least * (number_of - 1)
    while surplus > 0:
        movable = [i for i in range(1, number_of) if counts[i] < largest] or [i for i in range(1, number_of) if counts[i] < limit]
        whole, budget = sum([loads[i] for i in movable]), surplus
        for i in movable:
            more = min(limit - counts[i], max(1, budget * loads[i] // whole), surplus)
            counts[i] = counts[i] + more
            surplus = surplus - more
    return np.array(counts)


def gaussian(key, dims, scale, most, split=(), held_as=jnp.bfloat16):
    drawn = jax.random.normal(key, dims, jnp.float32) * scale
    if len(split) > 0:
        drawn = steps_of(key, dims, split, -0.22, 0.18) * drawn
    return jnp.clip(drawn, min=-most, max=most).astype(held_as)


def setup_inputs(seed: int = 0) -> dict:
    keys = jax.random.split(jax.random.key(seed), 15)
    w_obs = gaussian(keys[0], (M, NOBS), 1.0, 6.0, ((1, 128),), jnp.float32)
    r_obs = draw_r_obs(jax.random.fold_in(keys[14], 71), 0)
    p_obs = draw_p_obs(jax.random.fold_in(keys[14], 71), 0)
    obs_dest_keys = jax.random.split(jax.random.fold_in(keys[3], 1), NOBS // OBS_DEV)
    obs_dest_turns = jax.random.permutation(jax.random.fold_in(keys[3], 3), NOBS // OBS_DEV)
    obs_dest = jax.vmap(lambda own, number: assign_block(jax.random.fold_in(keys[3], 2), own, number, OBS_DEV, DEVICES, 1, CAP, 2))(obs_dest_keys, obs_dest_turns).reshape((NOBS, 1))
    obs_row = touch_ends(jax.random.randint(keys[4], (NOBS,), 0, CLAT - 1), jax.random.fold_in(keys[4], 1), 0, (CLAT - 1) - 1).astype(jnp.int32)
    obs_col = touch_ends(jax.random.randint(keys[5], (NOBS,), 0, CLON - 1), jax.random.fold_in(keys[5], 1), 0, (CLON - 1) - 1).astype(jnp.int32)
    obs_level = touch_ends(jax.random.randint(keys[6], (NOBS,), 0, LEV), jax.random.fold_in(keys[6], 1), 0, LEV - 1).astype(jnp.int32)
    obs_field = touch_ends(jax.random.randint(keys[7], (NOBS,), 0, F), jax.random.fold_in(keys[7], 1), 0, F - 1).astype(jnp.int32)
    obs_frac = jnp.clip(1.0 * jax.random.uniform(keys[8], (2, NOBS), jnp.float32) ** steps_of(keys[8], (2, NOBS), ((1, 128),), -0.2, 0.2), 0.0, 1.0)
    obs_var = jnp.clip(jnp.exp(math.log(2.0) - 1.3862944 * jax.random.uniform(keys[9], (NOBS,), jnp.float32) ** steps_of(keys[9], (NOBS,), ((0, 128),), -0.2, 0.2)), 0.5, 2.0)
    corr_panel = draw_corr_panel(jax.random.fold_in(keys[14], 71), 0)
    sigma_b = jnp.clip(jnp.exp(math.log(2.0) - 1.3862944 * jax.random.uniform(keys[11], (F, LEV, LAT, LON), jnp.float32) ** steps_of(keys[11], (F, LEV, LAT, LON), ((2, 8), (3, 16)), -0.2, 0.2)), 0.5, 2.0)
    coef_lat = jnp.clip(0.02 + 0.22 * jax.random.uniform(keys[12], (F, LEV, LAT, LON), jnp.float32) ** steps_of(keys[12], (F, LEV, LAT, LON), ((2, 8), (3, 16)), -0.2, 0.2), 0.02, 0.24)
    coef_lon = jnp.clip(0.02 + 0.22 * jax.random.uniform(keys[13], (F, LEV, LAT, LON), jnp.float32) ** steps_of(keys[13], (F, LEV, LAT, LON), ((2, 8), (3, 16)), -0.2, 0.2), 0.02, 0.24)
    return dict(w_obs=w_obs, r_obs=r_obs, p_obs=p_obs, obs_dest=obs_dest, obs_row=obs_row, obs_col=obs_col, obs_level=obs_level, obs_field=obs_field, obs_frac=obs_frac, obs_var=obs_var, corr_panel=corr_panel, sigma_b=sigma_b, coef_lat=coef_lat, coef_lon=coef_lon)


def diffuse(field_now, coef_lat, coef_lon):
    zero_row = jnp.zeros_like(field_now[..., :1, :])
    north_cells = jnp.concatenate([field_now[..., 1:, :], zero_row], axis=3)
    south_cells = jnp.concatenate([zero_row, field_now[..., :-1, :]], axis=3)
    lat_prev = jnp.concatenate([jnp.zeros_like(coef_lat[..., :1, :]), coef_lat[..., :-1, :]], axis=2)
    east_cells = jnp.roll(field_now, -1, axis=4)
    west_cells = jnp.roll(field_now, 1, axis=4)
    lon_prev = jnp.roll(coef_lon, 1, axis=3)
    return (field_now + coef_lat * (north_cells - field_now) - lat_prev * (field_now - south_cells)
            + coef_lon * (east_cells - field_now) - lon_prev * (field_now - west_cells))


def reference(w_obs, r_obs, p_obs, obs_dest, obs_row, obs_col, obs_level, obs_field, obs_frac, obs_var, corr_panel, sigma_b, coef_lat, coef_lon):
    destination = obs_dest[:, 0]
    lat_pos = (destination // N_LON) * CLAT + obs_row
    lon_pos = (destination % N_LON) * CLON + obs_col
    base_index = (((obs_field * LEV + obs_level) * LAT + lat_pos) * LON + lon_pos).astype(jnp.int32)
    lat_frac = obs_frac[0]
    lon_frac = obs_frac[1]
    offsets = (0, 1, LON, LON + 1)
    weights = ((1.0 - lat_frac) * (1.0 - lon_frac), (1.0 - lat_frac) * lon_frac, lat_frac * (1.0 - lon_frac), lat_frac * lon_frac)
    cell_count = F * LEV * LAT * LON
    adjoint_grid = jnp.zeros((M, cell_count), jnp.float32)
    for offset, weight in zip(offsets, weights):
        adjoint_grid = adjoint_grid.at[:, base_index + offset].add(weight[None, :] * p_obs)
    field_now = adjoint_grid.reshape(M, F, LEV, LAT, LON) * sigma_b
    for repeat in range(DSTEPS):
        field_now = diffuse(field_now, coef_lat, coef_lon)
    spread = (field_now * sigma_b).reshape(M, cell_count)
    forward = jnp.zeros((M, NOBS), jnp.float32)
    for offset, weight in zip(offsets, weights):
        forward = forward + weight[None, :] * spread[:, base_index + offset]
    p_round = p_obs.reshape(M, N_LAT, N_LON, OBS_DEV)[..., :RC].astype(jnp.bfloat16)
    corr_vector = jnp.transpose(p_round, (0, 2, 1, 3)).reshape(M, N_LON, N_LAT * RC).astype(jnp.float32)
    corr_term = jnp.einsum("jab,mjb->mja", corr_panel.astype(jnp.float32), corr_vector, precision=lax.Precision.HIGHEST)
    corr_term = jnp.transpose(corr_term.reshape(M, N_LON, N_LAT, RC), (0, 2, 1, 3))
    corr_full = jnp.zeros((M, N_LAT, N_LON, OBS_DEV), jnp.float32).at[..., :RC].set(corr_term).reshape(M, NOBS)
    applied = forward + obs_var[None, :] * p_obs + corr_full
    curvature = jnp.sum(p_obs * applied, axis=1)
    norm_old = jnp.sum(r_obs * r_obs, axis=1)
    step_size = norm_old / curvature
    w_next = w_obs + step_size[:, None] * p_obs
    r_next = r_obs - step_size[:, None] * applied
    norm_new = jnp.sum(r_next * r_next, axis=1)
    p_next = r_next + (norm_new / norm_old)[:, None] * p_obs
    return (w_next, r_next, p_next)
```

```python
import functools

import jax
import jax.numpy as jnp
from jax import lax
from jax.experimental import pallas as pl
from jax.experimental.pallas import tpu as pltpu
from jax.sharding import PartitionSpec as P

F32 = jnp.float32
BF16 = jnp.bfloat16
HIGHEST = lax.Precision.HIGHEST
DSTEPS = 4
RIM = 4
SLOT = 32
NT = (((1,), (1,)), ((), ()))
NN = (((1,), (0,)), ((), ()))
BLOCK = 512
RANKS_AT_ONCE = 8
MIB = 1024 * 1024


def dot(a, b, dims=NN, precision=None):
    return lax.dot_general(a, b, dims, precision=precision, preferred_element_type=F32)


def iota(shape, dim):
    return lax.broadcasted_iota(jnp.int32, shape, dim)


def call(kernel, out_shape, vmem, flops, moved, scratch=()):
    return pl.pallas_call(
        kernel,
        out_shape=out_shape,
        scratch_shapes=list(scratch),
        compiler_params=pltpu.CompilerParams(vmem_limit_bytes=vmem * MIB),
        cost_estimate=pl.CostEstimate(flops=flops, bytes_accessed=moved, transcendentals=0),
    )


def pack_kernel(
    levels, rows, columns, cap,
    p_ref, frac_ref, dest_ref, row_ref, col_ref, level_ref, field_ref, send_ref, rank_ref,
):
    peers = send_ref.shape[0]
    count = p_ref.shape[1]
    order = (iota((BLOCK, BLOCK), 0) < iota((BLOCK, BLOCK), 1)).astype(BF16)
    before = jnp.zeros((peers, 1), F32)
    total = jnp.zeros((peers, 6 * cap), F32)
    for start in range(0, count, BLOCK):
        at = slice(start, start + BLOCK)
        hot = (iota((peers, BLOCK), 0) == dest_ref[:, at]).astype(F32)
        hot16 = hot.astype(BF16)
        counts = dot(hot16, order) + before
        rank = jnp.sum(hot * counts, axis=0, keepdims=True)
        before = before + jnp.sum(hot, axis=1, keepdims=True)
        rank_ref[:, at] = rank
        rank_hot = (iota((cap, BLOCK), 0) == rank.astype(jnp.int32)).astype(F32)
        slab = field_ref[:, at] * levels + level_ref[:, at]
        cell = (slab * rows + row_ref[:, at]) * columns + col_ref[:, at]
        high = ((cell >> 9) - 256).astype(F32)
        low = ((cell & 511) - 256).astype(F32)
        frac = jnp.floor(frac_ref[:, at] * 256.0 + 0.5) * (1.0 / 256.0)
        p = p_ref[:, at]
        values = (p[0:1], p[1:2], frac[0:1], frac[1:2], high, low)
        payload = jnp.concatenate([(rank_hot * v).astype(BF16) for v in values], axis=0)
        total = total + dot(hot16, payload, NT)
    lane = iota((8, 128), 1)
    first = jnp.broadcast_to(p_ref[0:1, 0:128], (8, 128))
    second = pltpu.roll(jnp.broadcast_to(p_ref[1:2, 0:128], (8, 128)), 64, 1)
    corr = jnp.where(lane < 64, first, second)[0:1]
    pieces = [total[:, 128 * i : 128 * (i + 1)] for i in range(3)]
    pieces.append(jnp.broadcast_to(corr, (peers, 128)))
    send_ref[...] = jnp.stack(pieces, axis=1).astype(BF16)


def fill_rows(rows_ref, slot_ref, k, slabs, rows):
    for i in range(RANKS_AT_ONCE):
        lat_frac = slot_ref[2, pl.ds(k + i, 1), :]
        slab = slot_ref[4, pl.ds(k + i, 1), :]
        row = slot_ref[5, pl.ds(k + i, 1), :].astype(jnp.int32)
        index = iota((rows, 128), 0)
        weight = jnp.where(
            index == row, 1.0 - lat_frac, jnp.where(index == row + 1, lat_frac, 0.0)
        ).astype(BF16)
        for j in range(slabs):
            mask = (jnp.broadcast_to(slab, (16, 128)) == float(j)).astype(F32).astype(BF16)
            mask = jnp.concatenate([mask] * (rows // 16), axis=0)
            rows_ref[rows * j : rows * (j + 1), 128 * i : 128 * (i + 1)] = weight * mask


def column_weights(slot_ref, k, columns):
    lon_frac = slot_ref[3, pl.ds(k, 1), :]
    col = slot_ref[6, pl.ds(k, 1), :].astype(jnp.int32)
    index = iota((columns, 128), 0)
    return jnp.where(index == col, 1.0 - lon_frac, jnp.where(index == col + 1, lon_frac, 0.0))


def scatter_kernel(
    recv_ref, sigma_ref, field_ref, north_ref, south_ref, slot_ref, rows_ref, cols_ref, acc_ref
):
    slabs, rows, columns = sigma_ref.shape
    cap = slot_ref.shape[1]
    recv = recv_ref[...].astype(F32)
    parts = [recv[:, i, :].T for i in range(3)]
    slot_ref[0] = parts[0][:cap]
    slot_ref[1] = parts[0][cap:]
    slot_ref[2] = parts[1][:cap]
    slot_ref[3] = parts[1][cap:]
    high = parts[2][:cap].astype(jnp.int32) + 256
    low = parts[2][cap:].astype(jnp.int32) + 256
    cell = high * 512 + low
    slot_ref[4] = (cell >> 13).astype(F32)
    slot_ref[5] = ((cell >> 7) & 63).astype(F32)
    slot_ref[6] = (cell & 127).astype(F32)
    acc_ref[...] = jnp.zeros_like(acc_ref)

    def body(step, _):
        k = step * RANKS_AT_ONCE
        fill_rows(rows_ref, slot_ref, k, slabs, rows)
        for i in range(RANKS_AT_ONCE):
            weight = column_weights(slot_ref, k + i, columns)
            for m in range(2):
                p = slot_ref[m, pl.ds(k + i, 1), :]
                cols_ref[columns * m : columns * (m + 1), 128 * i : 128 * (i + 1)] = (
                    weight * p
                ).astype(BF16)
        acc_ref[...] += dot(rows_ref[...], cols_ref[...], NT)
        return 0

    lax.fori_loop(0, cap // RANKS_AT_ONCE, body, 0)
    for j in range(slabs):
        for m in range(2):
            part = acc_ref[rows * j : rows * (j + 1), columns * m : columns * (m + 1)]
            part = part * sigma_ref[j]
            field_ref[m * slabs + j] = part
            north_ref[m * slabs + j] = part[rows - RIM :]
            south_ref[m * slabs + j] = part[:RIM]


def with_rim(main, from_north, from_south):
    return jnp.concatenate([main, from_north, from_south], axis=0)


def strip_selector(columns):
    c = iota((4 * columns, 128), 0)
    lane = iota((4 * columns, 128), 1)
    place = lane % SLOT
    wanted = jnp.where(place < 8, columns - 8 + place, jnp.where(place >= 16, place - 16, -1))
    wanted = jnp.where(place >= 24, -1, wanted)
    return jnp.logical_and(c // columns == lane // SLOT, c % columns == wanted).astype(F32)


def dense_selector(group, first):
    lane = iota((128, 128), 0)
    n = iota((128, 128), 1)
    slab = n // RIM == 4 * group + lane // SLOT
    return jnp.logical_and(slab, lane % SLOT == first + n % RIM).astype(F32)


def rim_selector(group):
    n = iota((256, 128), 0)
    lane = iota((256, 128), 1)
    slab = (n % 128) // RIM == 4 * group + lane // SLOT
    return jnp.logical_and(slab, lane % SLOT == jnp.where(n < 128, 8, 12) + n % RIM).astype(F32)


def strip_kernel(main_ref, north_ref, south_ref, strip_ref, east_ref, west_ref):
    columns = main_ref.shape[2]
    select = strip_selector(columns)
    for a in range(east_ref.shape[0]):
        east = jnp.zeros(east_ref.shape[1:], F32)
        west = jnp.zeros(east_ref.shape[1:], F32)
        for g in range(8):
            at = 32 * a + 4 * g
            four = [with_rim(main_ref[at + i], north_ref[at + i], south_ref[at + i]) for i in range(4)]
            strip = dot(jnp.concatenate(four, axis=1), select, NN, HIGHEST)
            strip_ref[8 * a + g] = strip
            east = east + dot(strip, dense_selector(g, 4), NN, HIGHEST)
            west = west + dot(strip, dense_selector(g, 16), NN, HIGHEST)
        east_ref[a] = east
        west_ref[a] = west


def diffuse(fields, lat_coef, lon_coef, at_north):
    size, width = lat_coef.shape
    lat_prev = pltpu.roll(lat_coef, 1, 0)
    edge = jnp.logical_and(iota((8, width), 0) == 0, at_north)
    tail = jnp.where(edge, 0.0, lat_prev[size - 8 :])
    lat_prev = jnp.concatenate([lat_prev[: size - 8], tail], axis=0)
    lon_prev = pltpu.roll(lon_coef, 1, 1)
    centre = 1.0 - lat_coef - lat_prev - lon_coef - lon_prev
    results = []
    for h in fields:
        for _ in range(DSTEPS):
            h = (
                centre * h
                + lat_coef * pltpu.roll(h, size - 1, 0)
                + lat_prev * pltpu.roll(h, 1, 0)
                + lon_coef * pltpu.roll(h, width - 1, 1)
                + lon_prev * pltpu.roll(h, 1, 1)
            )
        results.append(h)
    return results


def main_kernel(
    place_ref, field_ref, north_ref, south_ref, lat_ref, lon_ref, cnorth_ref, csouth_ref, out_ref
):
    slabs, rows, _ = lat_ref.shape
    at_north = place_ref[0] == 1

    def body(j, _):
        lat_coef = with_rim(lat_ref[j], cnorth_ref[j], csouth_ref[j])
        lon_coef = with_rim(lon_ref[j], cnorth_ref[slabs + j], csouth_ref[slabs + j])
        at = [m * slabs + j for m in range(2)]
        fields = [with_rim(field_ref[i], north_ref[i], south_ref[i]) for i in at]
        for i, h in zip(at, diffuse(fields, lat_coef, lon_coef, at_north)):
            out_ref[i] = h[:rows]
        return 0

    lax.fori_loop(0, slabs, body, 0)


def gather_kernel(
    place_ref, strip_ref, east_ref, west_ref, cstrip_ref, ceast_ref, cwest_ref,
    main_ref, sigma_ref, slot_ref, back_ref, grid_ref, rows_ref, back_scr,
):
    slabs, rows, columns = sigma_ref.shape
    cap = slot_ref.shape[1]
    at_north = place_ref[0] == 1
    rims = [jnp.concatenate([east_ref[m], west_ref[m]], axis=1) for m in range(2)]
    crims = [jnp.concatenate([ceast_ref[m], cwest_ref[m]], axis=1) for m in range(2)]
    lane = iota((128, 4 * columns), 0)
    c = iota((128, 4 * columns), 1)
    wanted = jnp.where(
        c % columns < RIM, 16 + c % columns, jnp.where(c % columns >= columns - RIM, c % columns - (columns - 8), -1)
    )
    spread = jnp.logical_and(lane // SLOT == c // columns, lane % SLOT == wanted).astype(F32)
    column = iota((rows, columns), 1)
    inner = jnp.logical_and(column >= RIM, column < columns - RIM)
    for g in range(8):
        put = rim_selector(g)
        lat_coef = cstrip_ref[g] + dot(crims[0], put, NN, HIGHEST)
        lon_coef = cstrip_ref[8 + g] + dot(crims[1], put, NN, HIGHEST)
        fields = [strip_ref[8 * m + g] + dot(rims[m], put, NN, HIGHEST) for m in range(2)]
        for m, h in enumerate(diffuse(fields, lat_coef, lon_coef, at_north)):
            outer = dot(h[:rows], spread, NN, HIGHEST)
            for i in range(4):
                j = 4 * g + i
                whole = jnp.where(
                    inner, main_ref[m * slabs + j], outer[:, columns * i : columns * (i + 1)]
                )
                whole = whole * sigma_ref[j]
                grid_ref[rows * j : rows * (j + 1), columns * m : columns * (m + 1)] = whole
    grid = grid_ref[...].T.astype(BF16)

    def body(step, _):
        k = step * RANKS_AT_ONCE
        fill_rows(rows_ref, slot_ref, k, slabs, rows)
        picked = dot(grid, rows_ref[...])
        for i in range(RANKS_AT_ONCE):
            weight = column_weights(slot_ref, k + i, columns)
            for m in range(2):
                part = picked[columns * m : columns * (m + 1), 128 * i : 128 * (i + 1)]
                back_scr[pl.ds(cap * m + k + i, 1), :] = jnp.sum(part * weight, axis=0, keepdims=True)
        return 0

    lax.fori_loop(0, cap // RANKS_AT_ONCE, body, 0)
    back_ref[...] = back_scr[...].T.astype(BF16)


def unpack_kernel(
    place_ref, back_ref, recv_ref, dest_ref, rank_ref, p_ref, r_ref, var_ref, panel_ref,
    applied_ref, sums_ref,
):
    peers = back_ref.shape[0]
    cap = back_ref.shape[1] // 2
    count = p_ref.shape[1]
    lat_count = panel_ref.shape[1] // cap
    lon_count = peers // lat_count
    recv = recv_ref[...].astype(F32)[:, 3, :].astype(BF16)
    mine = iota((16, peers), 1) == iota((16, peers), 0) * lon_count + place_ref[1]
    group = dot(mine.astype(F32).astype(BF16), recv)
    corr = jnp.zeros((2, cap), F32)
    for i in range(lat_count):
        pair = jnp.concatenate([group[i : i + 1, :cap], group[i : i + 1, cap:]], axis=0)
        corr = corr + dot(pair.astype(BF16), panel_ref[:, cap * i : cap * (i + 1)], NT)
    corr = jnp.concatenate([corr, jnp.zeros((2, BLOCK - cap), F32)], axis=1)
    back = back_ref[...].astype(F32).T.astype(BF16)
    sums = [jnp.zeros((2, BLOCK), F32) for _ in range(4)]
    for start in range(0, count, BLOCK):
        at = slice(start, start + BLOCK)
        hot = (iota((peers, BLOCK), 0) == dest_ref[:, at]).astype(F32).astype(BF16)
        rank_hot = (iota((cap, BLOCK), 0) == rank_ref[:, at].astype(jnp.int32)).astype(F32)
        values = dot(back, hot)
        forward = [
            jnp.sum(values[cap * m : cap * (m + 1)] * rank_hot, axis=0, keepdims=True)
            for m in range(2)
        ]
        p = p_ref[:, at]
        r = r_ref[:, at]
        applied = jnp.concatenate(forward, axis=0) + var_ref[:, at] * p
        if start == 0:
            applied = applied + corr
        applied_ref[:, at] = applied
        for i, product in enumerate((p * applied, r * r, r * applied, applied * applied)):
            sums[i] = sums[i] + product
    lane = iota((2, 128), 1)
    row = iota((2, 128), 0)
    out = jnp.zeros((2, 128), F32)
    for i in range(4):
        total = jnp.sum(sums[i], axis=1, keepdims=True)
        out = out + jnp.where(lane == 2 * i + row, total, 0.0)
    sums_ref[...] = jnp.broadcast_to(jnp.sum(out, axis=0, keepdims=True), (peers, 128))


def update_kernel(sums_ref, applied_ref, w_ref, r_ref, p_ref, w_out, r_out, p_out):
    sums = jnp.sum(sums_ref[...], axis=0, keepdims=True)
    for m in range(2):
        at = slice(m, m + 1)
        curvature, norm_old, cross, square = (
            sums[:, 2 * i + m : 2 * i + m + 1] for i in range(4)
        )
        step = norm_old / curvature
        norm_new = norm_old - 2.0 * step * cross + step * step * square
        p = p_ref[at]
        r_next = r_ref[at] - step * applied_ref[at]
        w_out[at] = w_ref[at] + step * p
        r_out[at] = r_next
        p_out[at] = r_next + (norm_new / norm_old) * p


def shift(value, axis, steps, periodic):
    count = lax.axis_size(axis)
    pairs = [(i, (i + steps) % count) for i in range(count) if periodic or 0 <= i + steps < count]
    return lax.ppermute(value, axis, pairs)


def exchange(array):
    return lax.all_to_all(array, ("lat", "lon"), split_axis=0, concat_axis=0, tiled=True)


def local(
    w_obs, r_obs, p_obs, obs_dest, obs_row, obs_col, obs_level, obs_field, obs_frac, obs_var,
    corr_panel, sigma_b, coef_lat, coef_lon,
):
    lat_count = lax.axis_size("lat")
    lon_count = lax.axis_size("lon")
    peers = lat_count * lon_count
    count = p_obs.shape[1]
    cap = 2 * count // peers
    fields, levels, rows, columns = sigma_b.shape
    slabs = fields * levels
    shape = jax.ShapeDtypeStruct
    place = jnp.stack(
        [(lax.axis_index("lat") == lat_count - 1).astype(jnp.int32), lax.axis_index("lon")]
    ).astype(jnp.int32)
    smem = pl.BlockSpec(memory_space=pltpu.SMEM)
    vmem = pl.BlockSpec(memory_space=pltpu.VMEM)

    sigma = sigma_b.reshape(slabs, rows, columns)
    lat_coef = coef_lat.reshape(slabs, rows, columns)
    lon_coef = coef_lon.reshape(slabs, rows, columns)
    coefs = jnp.concatenate([lat_coef, lon_coef], axis=0)
    coef_south = shift(coefs[:, rows - RIM :], "lat", 1, False)
    coef_north = shift(coefs[:, :RIM], "lat", -1, False)
    ext = rows + 2 * RIM

    def strips(main, north, south):
        arrays = main.shape[0] // slabs
        return call(
            strip_kernel,
            (
                shape((8 * arrays, ext, 128), F32),
                shape((arrays, ext, 128), F32),
                shape((arrays, ext, 128), F32),
            ),
            24, 2_000_000_000, 4_000_000,
        )(main, north, south)

    cstrip, ceast, cwest = strips(coefs, coef_north, coef_south)
    ceast = shift(ceast, "lon", 1, True)
    cwest = shift(cwest, "lon", -1, True)

    line = lambda a: a.reshape(1, count)
    dest = line(obs_dest)
    send, rank = call(
        functools.partial(pack_kernel, levels, rows, columns, cap),
        (shape((peers, 4, 128), BF16), shape((1, count), F32)),
        24, 2_000_000_000, 500_000,
    )(p_obs, obs_frac, dest, line(obs_row), line(obs_col), line(obs_level), line(obs_field))
    recv = exchange(send)

    width = 128 * RANKS_AT_ONCE
    field, to_north, to_south, slot = call(
        scatter_kernel,
        (
            shape((2 * slabs, rows, columns), F32),
            shape((2 * slabs, RIM, columns), F32),
            shape((2 * slabs, RIM, columns), F32),
            shape((7, cap, peers), F32),
        ),
        32, 9_000_000_000, 4_000_000,
        (
            pltpu.VMEM((slabs * rows, width), BF16),
            pltpu.VMEM((2 * columns, width), BF16),
            pltpu.VMEM((slabs * rows, 2 * columns), F32),
        ),
    )(recv, sigma)
    south = shift(to_north, "lat", 1, False)
    north = shift(to_south, "lat", -1, False)
    strip, east, west = strips(field, north, south)
    east = shift(east, "lon", 1, True)
    west = shift(west, "lon", -1, True)

    done = pl.pallas_call(
        main_kernel,
        out_shape=shape((2 * slabs, rows, columns), F32),
        in_specs=[smem] + [vmem] * 7,
        out_specs=vmem,
        compiler_params=pltpu.CompilerParams(vmem_limit_bytes=24 * MIB),
        cost_estimate=pl.CostEstimate(flops=5_000_000_000, bytes_accessed=8_000_000, transcendentals=0),
    )(place, field, north, south, lat_coef, lon_coef, coef_north, coef_south)

    back = pl.pallas_call(
        gather_kernel,
        out_shape=shape((peers, 2 * cap), BF16),
        in_specs=[smem] + [vmem] * 9,
        out_specs=vmem,
        scratch_shapes=[
            pltpu.VMEM((slabs * rows, 2 * columns), F32),
            pltpu.VMEM((slabs * rows, width), BF16),
            pltpu.VMEM((2 * cap, peers), F32),
        ],
        compiler_params=pltpu.CompilerParams(vmem_limit_bytes=36 * MIB),
        cost_estimate=pl.CostEstimate(flops=9_000_000_000, bytes_accessed=8_000_000, transcendentals=0),
    )(place, strip, west, east, cstrip, cwest, ceast, done, sigma, slot)
    back = exchange(back)

    applied, sums = pl.pallas_call(
        unpack_kernel,
        out_shape=(shape((2, count), F32), shape((peers, 128), F32)),
        in_specs=[smem] + [vmem] * 8,
        out_specs=(vmem, vmem),
        compiler_params=pltpu.CompilerParams(vmem_limit_bytes=16 * MIB),
        cost_estimate=pl.CostEstimate(flops=300_000_000, bytes_accessed=500_000, transcendentals=0),
    )(place, back, recv, dest, rank, p_obs, r_obs, line(obs_var), corr_panel[0].T)
    sums = exchange(sums)
    whole = shape((2, count), F32)
    return call(update_kernel, (whole, whole, whole), 8, 100_000, 300_000)(
        sums, applied, w_obs, r_obs, p_obs
    )


def solution(mesh):
    both = ("lat", "lon")
    row = P(None, both)
    grid = P(None, None, "lat", "lon")
    in_specs = (
        row, row, row, P(both, None), P(both), P(both), P(both), P(both), row, P(both),
        P("lon", None, "lat"), grid, grid, grid,
    )
    return jax.shard_map(local, mesh=mesh, in_specs=in_specs, out_specs=(row, row, row), check_vma=False)
```

```python
import functools

import jax
import jax.numpy as jnp
from jax import lax
from jax.experimental import pallas as pl
from jax.experimental.pallas import tpu as pltpu
from jax.sharding import PartitionSpec as P

F32 = jnp.float32
BF16 = jnp.bfloat16
DSTEPS = 4
RIM = 4
SLOT = 32
NT = (((1,), (1,)), ((), ()))
NN = (((1,), (0,)), ((), ()))
BLOCK = 512
RANKS_AT_ONCE = 8
MIB = 1024 * 1024


def dot(a, b, dims=NN):
    return lax.dot_general(a, b, dims, preferred_element_type=F32)


def iota(shape, dim):
    return lax.broadcasted_iota(jnp.int32, shape, dim)


def call(kernel, out_shape, vmem, flops, moved, scratch=()):
    return pl.pallas_call(
        kernel,
        out_shape=out_shape,
        scratch_shapes=list(scratch),
        compiler_params=pltpu.CompilerParams(vmem_limit_bytes=vmem * MIB),
        cost_estimate=pl.CostEstimate(flops=flops, bytes_accessed=moved, transcendentals=0),
    )


def pack_kernel(
    levels, rows, columns, cap,
    p_hbm, frac_hbm, dest_hbm, row_hbm, col_hbm, level_hbm, field_hbm, send_ref, rank_ref,
    p_ref, frac_ref, dest_ref, row_ref, col_ref, level_ref, field_ref, sems,
):
    sources = (p_hbm, frac_hbm, dest_hbm, row_hbm, col_hbm, level_hbm, field_hbm)
    targets = (p_ref, frac_ref, dest_ref, row_ref, col_ref, level_ref, field_ref)
    copies = [
        pltpu.make_async_copy(source, target, sems.at[i])
        for i, (source, target) in enumerate(zip(sources, targets))
    ]
    for copy in copies:
        copy.start()
    for copy in copies:
        copy.wait()
    peers = send_ref.shape[0]
    count = p_ref.shape[1]
    order = (iota((BLOCK, BLOCK), 0) < iota((BLOCK, BLOCK), 1)).astype(BF16)
    before = jnp.zeros((peers, 1), F32)
    total = jnp.zeros((peers, 6 * cap), F32)
    for start in range(0, count, BLOCK):
        at = slice(start, start + BLOCK)
        hot = (iota((peers, BLOCK), 0) == dest_ref[:, at]).astype(F32)
        hot16 = hot.astype(BF16)
        counts = dot(hot16, order) + before
        rank = jnp.sum(hot * counts, axis=0, keepdims=True)
        before = before + jnp.sum(hot, axis=1, keepdims=True)
        rank_ref[:, at] = rank
        rank_hot = (iota((cap, BLOCK), 0) == rank.astype(jnp.int32)).astype(F32)
        slab = field_ref[:, at] * levels + level_ref[:, at]
        cell = (slab * rows + row_ref[:, at]) * columns + col_ref[:, at]
        high = ((cell >> 9) - 256).astype(F32)
        low = ((cell & 511) - 256).astype(F32)
        frac = jnp.floor(frac_ref[:, at] * 256.0 + 0.5) * (1.0 / 256.0)
        p = p_ref[:, at]
        values = (p[0:1], p[1:2], frac[0:1], frac[1:2], high, low)
        payload = jnp.concatenate([(rank_hot * v).astype(BF16) for v in values], axis=0)
        total = total + dot(hot16, payload, NT)
    lane = iota((8, 128), 1)
    first = jnp.broadcast_to(p_ref[0:1, 0:128], (8, 128))
    second = pltpu.roll(jnp.broadcast_to(p_ref[1:2, 0:128], (8, 128)), 64, 1)
    corr = jnp.where(lane < 64, first, second)[0:1]
    pieces = [total[:, 128 * i : 128 * (i + 1)] for i in range(3)]
    pieces.append(jnp.broadcast_to(corr, (peers, 128)))
    send_ref[...] = jnp.stack(pieces, axis=1).astype(BF16)


def fill_rows(rows_ref, slot_ref, k, slabs, rows):
    for i in range(RANKS_AT_ONCE):
        lat_frac = slot_ref[2, pl.ds(k + i, 1), :]
        slab = slot_ref[4, pl.ds(k + i, 1), :]
        row = slot_ref[5, pl.ds(k + i, 1), :].astype(jnp.int32)
        index = iota((rows, 128), 0)
        weight = jnp.where(
            index == row, 1.0 - lat_frac, jnp.where(index == row + 1, lat_frac, 0.0)
        ).astype(BF16)
        none = jnp.zeros((rows, 128), BF16)
        slab = jnp.broadcast_to(slab, (rows, 128)).astype(BF16)
        for j in range(slabs):
            at = slice(rows * j, rows * (j + 1))
            rows_ref[at, 128 * i : 128 * (i + 1)] = jnp.where(slab == j, weight, none)


def column_weights(slot_ref, k, columns):
    lon_frac = slot_ref[3, pl.ds(k, 1), :]
    col = slot_ref[6, pl.ds(k, 1), :].astype(jnp.int32)
    index = iota((columns, 128), 0)
    return jnp.where(index == col, 1.0 - lon_frac, jnp.where(index == col + 1, lon_frac, 0.0))


def scatter_kernel(
    recv_ref, sigma_ref, field_ref, north_ref, south_ref, slot_ref, rows_ref, cols_ref, acc_ref
):
    slabs, rows, columns = sigma_ref.shape
    cap = slot_ref.shape[1]
    recv = recv_ref[...].astype(F32)
    parts = [recv[:, i, :].T for i in range(3)]
    slot_ref[0] = parts[0][:cap]
    slot_ref[1] = parts[0][cap:]
    slot_ref[2] = parts[1][:cap]
    slot_ref[3] = parts[1][cap:]
    high = parts[2][:cap].astype(jnp.int32) + 256
    low = parts[2][cap:].astype(jnp.int32) + 256
    cell = high * 512 + low
    slot_ref[4] = (cell >> 13).astype(F32)
    slot_ref[5] = ((cell >> 7) & 63).astype(F32)
    slot_ref[6] = (cell & 127).astype(F32)
    acc_ref[...] = jnp.zeros_like(acc_ref)

    def body(step, _):
        k = step * RANKS_AT_ONCE
        fill_rows(rows_ref, slot_ref, k, slabs, rows)
        for i in range(RANKS_AT_ONCE):
            weight = column_weights(slot_ref, k + i, columns)
            for m in range(2):
                p = slot_ref[m, pl.ds(k + i, 1), :]
                cols_ref[columns * m : columns * (m + 1), 128 * i : 128 * (i + 1)] = (
                    weight * p
                ).astype(BF16)
        acc_ref[...] += dot(rows_ref[...], cols_ref[...], NT)
        return 0

    lax.fori_loop(0, cap // RANKS_AT_ONCE, body, 0)
    for j in range(slabs):
        for m in range(2):
            part = acc_ref[rows * j : rows * (j + 1), columns * m : columns * (m + 1)]
            part = part * sigma_ref[j]
            field_ref[m * slabs + j] = part
            north_ref[m * slabs + j] = part[rows - RIM :]
            south_ref[m * slabs + j] = part[:RIM]


def with_rim(main, from_north, from_south):
    return jnp.concatenate([main, from_north, from_south], axis=0)


def strip_kernel(sources, *refs):
    inputs, outputs = refs[: sources + 2], refs[sources + 2 :]
    *inputs, north_ref, south_ref = inputs
    *more, strip_ref, east_ref, west_ref = outputs
    size = strip_ref.shape[1]
    lane = iota((size, 128), 1)
    place = lane % SLOT
    slabs = north_ref.shape[0] // 2
    east = [jnp.zeros((size, 128), F32)] * 2
    west = [jnp.zeros((size, 128), F32)] * 2
    for g in range(slabs // 4):
        for a in range(2):
            ref, first = (inputs[0], slabs * a) if sources == 1 else (inputs[a], 0)
            outer = jnp.zeros((size, 128), F32)
            for i in range(4):
                j = 4 * g + i
                x = with_rim(ref[first + j], north_ref[slabs * a + j], south_ref[slabs * a + j])
                outer = jnp.where(lane // SLOT == i, pltpu.roll(x, SLOT * i + 8, 1), outer)
            strip = jnp.where(place < 8, outer, pltpu.roll(outer, 8, 1))
            inside = jnp.logical_or(place < 8, jnp.logical_and(place >= 16, place < 24))
            strip_ref[slabs // 4 * a + g] = jnp.where(inside, strip, 0.0)
            mine = place // RIM == g
            east[a] = jnp.where(mine, pltpu.roll(outer, (RIM * g - 4) % 128, 1), east[a])
            west[a] = jnp.where(mine, pltpu.roll(outer, (RIM * g - 8) % 128, 1), west[a])
    for a in range(2):
        east_ref[a] = east[a]
        west_ref[a] = west[a]
    if more:
        east_ref[2:] = more[0][...]
        west_ref[2:] = more[1][...]


def coefs_of(lat_coef, lon_coef, at_south, at_north):
    size, width = lat_coef.shape
    row = iota((8, width), 0)
    lat_prev = pltpu.roll(lat_coef, 1, 0)
    head = jnp.where(jnp.logical_and(row == 0, at_south), 0.0, lat_prev[:8])
    lat_prev = jnp.concatenate([head, lat_prev[8:]], axis=0)
    lon_prev = pltpu.roll(lon_coef, 1, 1)
    centre = 1.0 - lat_coef - lat_prev - lon_coef - lon_prev
    last = jnp.where(jnp.logical_and(row == 7, at_north), 0.0, lat_coef[size - 16 : size - 8])
    lat_next = jnp.concatenate([lat_coef[: size - 16], last, lat_coef[size - 8 :]], axis=0)
    return centre, lat_next, lat_prev, lon_coef, lon_prev


def diffuse_step(h, coefs):
    size, width = h.shape
    centre, lat_coef, lat_prev, lon_coef, lon_prev = coefs
    return (
        centre * h
        + lat_coef * pltpu.roll(h, size - 1, 0)
        + lat_prev * pltpu.roll(h, 1, 0)
        + lon_coef * pltpu.roll(h, width - 1, 1)
        + lon_prev * pltpu.roll(h, 1, 1)
    )


def diffuse(fields, coefs):
    for _ in range(DSTEPS):
        fields = [[diffuse_step(h, c) for h in tiles] for tiles, c in zip(fields, coefs)]
    return fields


def main_kernel(
    place_ref, field_ref, north_ref, south_ref, lat_ref, lon_ref, cnorth_ref, csouth_ref, out_ref
):
    slabs, rows, _ = lat_ref.shape
    at_south, at_north = place_ref[0] == 1, place_ref[1] == 1

    def body(step, _):
        tiles = [4 * step + i for i in range(4)]
        coefs = [
            coefs_of(
                with_rim(lat_ref[j], cnorth_ref[j], csouth_ref[j]),
                with_rim(lon_ref[j], cnorth_ref[slabs + j], csouth_ref[slabs + j]),
                at_south,
                at_north,
            )
            for j in tiles
        ]
        fields = [
            [with_rim(field_ref[i], north_ref[i], south_ref[i]) for i in (j, slabs + j)]
            for j in tiles
        ]
        for j, results in zip(tiles, diffuse(fields, coefs)):
            for m in range(2):
                out_ref[m * slabs + j] = results[m][:rows]
        return 0

    lax.fori_loop(0, slabs // 4, body, 0)


def gather_kernel(
    place_ref, strip_ref, cstrip_ref, east_ref, west_ref,
    main_ref, sigma_ref, slot_ref, back_ref, grid_ref, rows_ref, back_scr,
):
    slabs, rows, columns = sigma_ref.shape
    cap = slot_ref.shape[1]
    groups = slabs // 4
    at_south, at_north = place_ref[0] == 1, place_ref[1] == 1
    size = strip_ref.shape[1]
    place = iota((size, 128), 1) % SLOT
    column = iota((rows, columns), 1)
    inner = jnp.logical_and(column >= RIM, column < columns - RIM)

    def joined(strip, east, west, g):
        east = pltpu.roll(east, (8 - RIM * g) % 128, 1)
        west = pltpu.roll(west, (12 - RIM * g) % 128, 1)
        return jnp.where(place // RIM == 2, east, jnp.where(place // RIM == 3, west, strip))

    for first in range(0, groups, 4):
        tiles = range(first, first + 4)
        coefs = [
            coefs_of(
                *(
                    joined(cstrip_ref[groups * a + g], east_ref[2 + a], west_ref[2 + a], g)
                    for a in range(2)
                ),
                at_south,
                at_north,
            )
            for g in tiles
        ]
        fields = [
            [joined(strip_ref[groups * m + g], east_ref[m], west_ref[m], g) for m in range(2)]
            for g in tiles
        ]
        for g, results in zip(tiles, diffuse(fields, coefs)):
            for m in range(2):
                h = results[m][:rows]
                outer = jnp.where(place[:rows] < 8, h, pltpu.roll(h, 120, 1))
                for i in range(4):
                    j = 4 * g + i
                    edges = pltpu.roll(outer, (120 - SLOT * i) % 128, 1)
                    whole = jnp.where(inner, main_ref[m * slabs + j], edges) * sigma_ref[j]
                    grid_ref[rows * j : rows * (j + 1), columns * m : columns * (m + 1)] = whole
    grid = grid_ref[...].T.astype(BF16)

    def body(step, _):
        k = step * RANKS_AT_ONCE
        fill_rows(rows_ref, slot_ref, k, slabs, rows)
        picked = dot(grid, rows_ref[...])
        for i in range(RANKS_AT_ONCE):
            weight = column_weights(slot_ref, k + i, columns)
            for m in range(2):
                part = picked[columns * m : columns * (m + 1), 128 * i : 128 * (i + 1)]
                back_scr[pl.ds(cap * m + k + i, 1), :] = jnp.sum(part * weight, axis=0, keepdims=True)
        return 0

    lax.fori_loop(0, cap // RANKS_AT_ONCE, body, 0)
    back_ref[...] = back_scr[...].T.astype(BF16)


def unpack_kernel(
    place_ref, back_ref, recv_ref, dest_ref, rank_ref, p_ref, r_ref, var_ref, panel_ref,
    applied_ref, sums_ref,
):
    peers = back_ref.shape[0]
    cap = back_ref.shape[1] // 2
    count = p_ref.shape[1]
    lat_count = panel_ref.shape[1] // cap
    lon_count = peers // lat_count
    recv = recv_ref[...].astype(F32)[:, 3, :].astype(BF16)
    mine = iota((16, peers), 1) == iota((16, peers), 0) * lon_count + place_ref[2]
    group = dot(mine.astype(F32).astype(BF16), recv)
    corr = jnp.zeros((2, cap), F32)
    for i in range(lat_count):
        pair = jnp.concatenate([group[i : i + 1, :cap], group[i : i + 1, cap:]], axis=0)
        corr = corr + dot(pair.astype(BF16), panel_ref[:, cap * i : cap * (i + 1)], NT)
    corr = jnp.concatenate([corr, jnp.zeros((2, BLOCK - cap), F32)], axis=1)
    back = back_ref[...].astype(F32).T.astype(BF16)
    sums = [jnp.zeros((2, BLOCK), F32) for _ in range(4)]
    for start in range(0, count, BLOCK):
        at = slice(start, start + BLOCK)
        hot = (iota((peers, BLOCK), 0) == dest_ref[:, at]).astype(F32).astype(BF16)
        rank_hot = (iota((cap, BLOCK), 0) == rank_ref[:, at].astype(jnp.int32)).astype(F32)
        values = dot(back, hot)
        forward = [
            jnp.sum(values[cap * m : cap * (m + 1)] * rank_hot, axis=0, keepdims=True)
            for m in range(2)
        ]
        p = p_ref[:, at]
        r = r_ref[:, at]
        applied = jnp.concatenate(forward, axis=0) + var_ref[:, at] * p
        if start == 0:
            applied = applied + corr
        applied_ref[:, at] = applied
        for i, product in enumerate((p * applied, r * r, r * applied, applied * applied)):
            sums[i] = sums[i] + product
    lane = iota((2, 128), 1)
    row = iota((2, 128), 0)
    out = jnp.zeros((2, 128), F32)
    for i in range(4):
        total = jnp.sum(sums[i], axis=1, keepdims=True)
        out = out + jnp.where(lane == 2 * i + row, total, 0.0)
    sums_ref[...] = jnp.broadcast_to(jnp.sum(out, axis=0, keepdims=True), (peers, 128))


def update_kernel(sums_ref, applied_ref, w_ref, r_ref, p_ref, w_out, r_out, p_out):
    sums = jnp.sum(sums_ref[...], axis=0, keepdims=True)
    for m in range(2):
        at = slice(m, m + 1)
        curvature, norm_old, cross, square = (
            sums[:, 2 * i + m : 2 * i + m + 1] for i in range(4)
        )
        step = norm_old / curvature
        norm_new = norm_old - 2.0 * step * cross + step * step * square
        p = p_ref[at]
        r_next = r_ref[at] - step * applied_ref[at]
        w_out[at] = w_ref[at] + step * p
        r_out[at] = r_next
        p_out[at] = r_next + (norm_new / norm_old) * p


def shift(value, axis, steps):
    count = lax.axis_size(axis)
    return lax.ppermute(value, axis, [(i, (i + steps) % count) for i in range(count)])


def exchange(array):
    return lax.all_to_all(array, ("lat", "lon"), split_axis=0, concat_axis=0, tiled=True)


def local(
    w_obs, r_obs, p_obs, obs_dest, obs_row, obs_col, obs_level, obs_field, obs_frac, obs_var,
    corr_panel, sigma_b, coef_lat, coef_lon,
):
    lat_count = lax.axis_size("lat")
    lon_count = lax.axis_size("lon")
    peers = lat_count * lon_count
    count = p_obs.shape[1]
    cap = 2 * count // peers
    fields, levels, rows, columns = sigma_b.shape
    slabs = fields * levels
    shape = jax.ShapeDtypeStruct
    place = jnp.stack(
        [
            (lax.axis_index("lat") == 0).astype(jnp.int32),
            (lax.axis_index("lat") == lat_count - 1).astype(jnp.int32),
            lax.axis_index("lon"),
        ]
    ).astype(jnp.int32)
    smem = pl.BlockSpec(memory_space=pltpu.SMEM)
    vmem = pl.BlockSpec(memory_space=pltpu.VMEM)
    hbm = pl.BlockSpec(memory_space=pltpu.HBM)

    sigma = sigma_b.reshape(slabs, rows, columns)
    lat_coef = coef_lat.reshape(slabs, rows, columns)
    lon_coef = coef_lon.reshape(slabs, rows, columns)
    edges = lambda at: jnp.concatenate([lat_coef[:, at], lon_coef[:, at]], axis=0)
    coef_south = shift(edges(slice(rows - RIM, None)), "lat", 1)
    coef_north = shift(edges(slice(0, RIM)), "lat", -1)
    ext = rows + 2 * RIM
    groups = slabs // 4

    def strips(sources, *arrays):
        outer = shape((len(arrays) - sources, ext, 128), F32)
        return call(
            functools.partial(strip_kernel, sources),
            (shape((2 * groups, ext, 128), F32), outer, outer),
            24, 500_000_000, 4_000_000,
        )(*arrays)

    cstrip, c_east, c_west = strips(2, lat_coef, lon_coef, coef_north, coef_south)

    line = lambda a: a.reshape(1, count)
    dest = line(obs_dest)
    pair = pltpu.VMEM((2, count), F32)
    single = pltpu.VMEM((1, count), jnp.int32)
    send, rank = pl.pallas_call(
        functools.partial(pack_kernel, levels, rows, columns, cap),
        out_shape=(shape((peers, 4, 128), BF16), shape((1, count), F32)),
        in_specs=[hbm] * 7,
        out_specs=(vmem, vmem),
        scratch_shapes=[pair, pair] + [single] * 5 + [pltpu.SemaphoreType.DMA((7,))],
        compiler_params=pltpu.CompilerParams(vmem_limit_bytes=56 * MIB),
        cost_estimate=pl.CostEstimate(flops=2_000_000_000, bytes_accessed=500_000, transcendentals=0),
    )(p_obs, obs_frac, dest, line(obs_row), line(obs_col), line(obs_level), line(obs_field))
    recv = exchange(send)

    width = 128 * RANKS_AT_ONCE
    field, to_north, to_south, slot = call(
        scatter_kernel,
        (
            shape((2 * slabs, rows, columns), F32),
            shape((2 * slabs, RIM, columns), F32),
            shape((2 * slabs, RIM, columns), F32),
            shape((7, cap, peers), F32),
        ),
        32, 9_000_000_000, 4_000_000,
        (
            pltpu.VMEM((slabs * rows, width), BF16),
            pltpu.VMEM((2 * columns, width), BF16),
            pltpu.VMEM((slabs * rows, 2 * columns), F32),
        ),
    )(recv, sigma)
    south = shift(to_north, "lat", 1)
    north = shift(to_south, "lat", -1)
    strip, to_east, to_west = strips(1, field, north, south, c_east, c_west)
    west = shift(to_east, "lon", 1)
    east = shift(to_west, "lon", -1)

    done = pl.pallas_call(
        main_kernel,
        out_shape=shape((2 * slabs, rows, columns), F32),
        in_specs=[smem] + [vmem] * 7,
        out_specs=vmem,
        compiler_params=pltpu.CompilerParams(vmem_limit_bytes=24 * MIB),
        cost_estimate=pl.CostEstimate(flops=5_000_000_000, bytes_accessed=8_000_000, transcendentals=0),
    )(place, field, north, south, lat_coef, lon_coef, coef_north, coef_south)

    back = pl.pallas_call(
        gather_kernel,
        out_shape=shape((peers, 2 * cap), BF16),
        in_specs=[smem] + [vmem] * 7,
        out_specs=vmem,
        scratch_shapes=[
            pltpu.VMEM((slabs * rows, 2 * columns), F32),
            pltpu.VMEM((slabs * rows, width), BF16),
            pltpu.VMEM((2 * cap, peers), F32),
        ],
        compiler_params=pltpu.CompilerParams(vmem_limit_bytes=36 * MIB),
        cost_estimate=pl.CostEstimate(flops=9_000_000_000, bytes_accessed=8_000_000, transcendentals=0),
    )(place, strip, cstrip, east, west, done, sigma, slot)
    back = exchange(back)

    applied, sums = pl.pallas_call(
        unpack_kernel,
        out_shape=(shape((2, count), F32), shape((peers, 128), F32)),
        in_specs=[smem] + [vmem] * 8,
        out_specs=(vmem, vmem),
        compiler_params=pltpu.CompilerParams(vmem_limit_bytes=16 * MIB),
        cost_estimate=pl.CostEstimate(flops=300_000_000, bytes_accessed=500_000, transcendentals=0),
    )(place, back, recv, dest, rank, p_obs, r_obs, line(obs_var), corr_panel[0].T)
    sums = exchange(sums)
    whole = shape((2, count), F32)
    return call(update_kernel, (whole, whole, whole), 8, 100_000, 300_000)(
        sums, applied, w_obs, r_obs, p_obs
    )


def solution(mesh):
    both = ("lat", "lon")
    row = P(None, both)
    grid = P(None, None, "lat", "lon")
    in_specs = (
        row, row, row, P(both, None), P(both), P(both), P(both), P(both), row, P(both),
        P("lon", None, "lat"), grid, grid, grid,
    )
    return jax.shard_map(local, mesh=mesh, in_specs=in_specs, out_specs=(row, row, row), check_vma=False)
```

```python
import functools

import jax
import jax.numpy as jnp
from jax import lax
from jax.experimental import pallas as pl
from jax.experimental.pallas import tpu as pltpu
from jax.sharding import PartitionSpec as P

F32 = jnp.float32
BF16 = jnp.bfloat16
DSTEPS = 4
RIM = 4
SLOT = 32
NT = (((1,), (1,)), ((), ()))
NN = (((1,), (0,)), ((), ()))
BLOCK = 512
PACK_BLOCK = 512
RANKS_AT_ONCE = 8
MIB = 1024 * 1024


def dot(a, b, dims=NN):
    return lax.dot_general(a, b, dims, preferred_element_type=F32)


def iota(shape, dim):
    return lax.broadcasted_iota(jnp.int32, shape, dim)


def call(kernel, out_shape, vmem, flops, moved, scratch=()):
    return pl.pallas_call(
        kernel,
        out_shape=out_shape,
        scratch_shapes=list(scratch),
        compiler_params=pltpu.CompilerParams(vmem_limit_bytes=vmem * MIB),
        cost_estimate=pl.CostEstimate(flops=flops, bytes_accessed=moved, transcendentals=0),
    )


def pack_kernel(
    half, levels, rows, columns, cap,
    p_hbm, frac_hbm, dest_hbm, row_hbm, col_hbm, level_hbm, field_hbm, send_ref, rank_ref,
    p_ref, frac_ref, dest_ref, row_ref, col_ref, level_ref, field_ref, sems,
):
    sources = (p_hbm, frac_hbm, dest_hbm, row_hbm, col_hbm, level_hbm, field_hbm)
    targets = (p_ref, frac_ref, dest_ref, row_ref, col_ref, level_ref, field_ref)
    copies = [
        pltpu.make_async_copy(source, target, sems.at[i])
        for i, (source, target) in enumerate(zip(sources, targets))
    ]
    for copy in copies:
        copy.start()
    for copy in copies:
        copy.wait()
    peers = send_ref.shape[0]
    count = p_ref.shape[1]
    order = (iota((PACK_BLOCK, PACK_BLOCK), 0) < iota((PACK_BLOCK, PACK_BLOCK), 1)).astype(BF16)
    before = jnp.zeros((2 * peers, 1), F32)
    total = jnp.zeros((peers, 6 * cap), F32)
    for start in range(0, count, PACK_BLOCK):
        at = slice(start, start + PACK_BLOCK)
        slab = field_ref[:, at] * levels + level_ref[:, at]
        upper = slab >= half
        key = jnp.where(upper, peers, 0) + dest_ref[:, at]
        hot = (iota((2 * peers, PACK_BLOCK), 0) == key).astype(F32)
        counts = dot(hot.astype(BF16), order) + before
        rank = jnp.sum(hot * counts, axis=0, keepdims=True)
        before = before + jnp.sum(hot, axis=1, keepdims=True)
        rank = jnp.where(upper, cap - 1.0 - rank, rank)
        hot16 = (hot[:peers] + hot[peers:]).astype(BF16)
        rank_ref[:, at] = rank
        rank_hot = (iota((cap, PACK_BLOCK), 0) == rank.astype(jnp.int32)).astype(F32)
        cell = (slab * rows + row_ref[:, at]) * columns + col_ref[:, at]
        high = cell >> 9
        high = (jnp.where(upper, high + 1, high) - 256).astype(F32)
        low = ((cell & 511) - 256).astype(F32)
        frac = jnp.floor(frac_ref[:, at] * 256.0 + 0.5) * (1.0 / 256.0)
        p = p_ref[:, at]
        values = (p[0:1], p[1:2], frac[0:1], frac[1:2], high, low)
        payload = jnp.concatenate([(rank_hot * v).astype(BF16) for v in values], axis=0)
        total = total + dot(hot16, payload, NT)
    lane = iota((8, 128), 1)
    first = jnp.broadcast_to(p_ref[0:1, 0:128], (8, 128))
    second = pltpu.roll(jnp.broadcast_to(p_ref[1:2, 0:128], (8, 128)), 64, 1)
    corr = jnp.where(lane < 64, first, second)[0:1]
    pieces = [total[:, 128 * i : 128 * (i + 1)] for i in range(3)]
    pieces.append(jnp.broadcast_to(corr, (peers, 128)))
    send_ref[...] = jnp.stack(pieces, axis=1).astype(BF16)


def fill_rows(rows_ref, slot_ref, k, first, slabs, rows):
    for i in range(RANKS_AT_ONCE):
        lat_frac = slot_ref[2, pl.ds(k + i, 1), :]
        slab = slot_ref[4, pl.ds(k + i, 1), :]
        row = slot_ref[5, pl.ds(k + i, 1), :].astype(jnp.int32)
        index = iota((rows, 128), 0)
        weight = jnp.where(
            index == row, 1.0 - lat_frac, jnp.where(index == row + 1, lat_frac, 0.0)
        ).astype(BF16)
        none = jnp.zeros((rows, 128), BF16)
        slab = jnp.broadcast_to(slab, (rows, 128)).astype(BF16)
        for j in range(slabs):
            at = slice(rows * j, rows * (j + 1))
            rows_ref[at, 128 * i : 128 * (i + 1)] = jnp.where(slab == first + j, weight, none)


def halves(flag_ref, k):
    code = flag_ref[0, k]
    for i in range(1, RANKS_AT_ONCE):
        code = code | flag_ref[0, k + i]
    return (code & 1) != 0, (code & 2) != 0


def branches(used, slabs):
    lower, upper = used
    half = slabs // 2
    return (
        (jnp.logical_and(lower, upper), 0, slabs),
        (jnp.logical_and(lower, jnp.logical_not(upper)), 0, half),
        (jnp.logical_and(upper, jnp.logical_not(lower)), half, half),
    )


def column_weights(slot_ref, k, columns):
    lon_frac = slot_ref[3, pl.ds(k, 1), :]
    col = slot_ref[6, pl.ds(k, 1), :].astype(jnp.int32)
    index = iota((columns, 128), 0)
    return jnp.where(index == col, 1.0 - lon_frac, jnp.where(index == col + 1, lon_frac, 0.0))


def scatter_kernel(
    recv_ref, sigma_ref, field_ref, north_ref, south_ref, slot_ref, flag_ref,
    rows_ref, cols_ref, acc_ref, code_ref, sem,
):
    slabs, rows, columns = sigma_ref.shape
    cap = slot_ref.shape[1]
    recv = recv_ref[...].astype(F32)
    cells = recv[:, 2, :]
    lower = (jnp.min(cells, axis=0, keepdims=True) < 0.0).astype(jnp.int32)
    upper = (jnp.max(cells, axis=0, keepdims=True) > 0.0).astype(jnp.int32)
    flag_ref[...] = lower + 2 * upper
    copy = pltpu.make_async_copy(flag_ref, code_ref, sem)
    copy.start()
    parts = [recv[:, i, :].T for i in range(3)]
    slot_ref[0] = parts[0][:cap]
    slot_ref[1] = parts[0][cap:]
    slot_ref[2] = parts[1][:cap]
    slot_ref[3] = parts[1][cap:]
    high = parts[2][:cap].astype(jnp.int32)
    high = jnp.where(high > 0, high - 1, high) + 256
    low = parts[2][cap:].astype(jnp.int32) + 256
    cell = high * 512 + low
    slot_ref[4] = (cell >> 13).astype(F32)
    slot_ref[5] = ((cell >> 7) & 63).astype(F32)
    slot_ref[6] = (cell & 127).astype(F32)
    acc_ref[...] = jnp.zeros_like(acc_ref)
    copy.wait()

    def body(step, _):
        k = step * RANKS_AT_ONCE
        used = halves(code_ref, k)

        for test, first, length in branches(used, slabs):

            @pl.when(test)
            def _():
                for i in range(RANKS_AT_ONCE):
                    weight = column_weights(slot_ref, k + i, columns)
                    for m in range(2):
                        p = slot_ref[m, pl.ds(k + i, 1), :]
                        cols_ref[columns * m : columns * (m + 1), 128 * i : 128 * (i + 1)] = (
                            weight * p
                        ).astype(BF16)
                fill_rows(rows_ref, slot_ref, k, first, length, rows)
                at = slice(rows * first, rows * (first + length))
                acc_ref[at] += dot(rows_ref[: rows * length], cols_ref[...], NT)

        return 0

    lax.fori_loop(0, cap // RANKS_AT_ONCE, body, 0)
    for j in range(slabs):
        for m in range(2):
            part = acc_ref[rows * j : rows * (j + 1), columns * m : columns * (m + 1)]
            part = part * sigma_ref[j]
            field_ref[m * slabs + j] = part
            north_ref[m * slabs + j] = part[rows - RIM :]
            south_ref[m * slabs + j] = part[:RIM]


def with_rim(main, from_north, from_south):
    return jnp.concatenate([main, from_north, from_south], axis=0)


def strip_kernel(sources, *refs):
    inputs, outputs = refs[: sources + 2], refs[sources + 2 :]
    *inputs, north_ref, south_ref = inputs
    *more, strip_ref, east_ref, west_ref = outputs
    size = strip_ref.shape[1]
    lane = iota((size, 128), 1)
    place = lane % SLOT
    slabs = north_ref.shape[0] // 2
    east = [jnp.zeros((size, 128), F32)] * 2
    west = [jnp.zeros((size, 128), F32)] * 2
    for g in range(slabs // 4):
        for a in range(2):
            ref, first = (inputs[0], slabs * a) if sources == 1 else (inputs[a], 0)
            outer = jnp.zeros((size, 128), F32)
            for i in range(4):
                j = 4 * g + i
                x = with_rim(ref[first + j], north_ref[slabs * a + j], south_ref[slabs * a + j])
                outer = jnp.where(lane // SLOT == i, pltpu.roll(x, SLOT * i + 8, 1), outer)
            strip = jnp.where(place < 8, outer, pltpu.roll(outer, 8, 1))
            inside = jnp.logical_or(place < 8, jnp.logical_and(place >= 16, place < 24))
            strip_ref[slabs // 4 * a + g] = jnp.where(inside, strip, 0.0)
            mine = place // RIM == g
            east[a] = jnp.where(mine, pltpu.roll(outer, (RIM * g - 4) % 128, 1), east[a])
            west[a] = jnp.where(mine, pltpu.roll(outer, (RIM * g - 8) % 128, 1), west[a])
    for a in range(2):
        east_ref[a] = east[a]
        west_ref[a] = west[a]
    if more:
        east_ref[2:] = more[0][...]
        west_ref[2:] = more[1][...]


def coefs_of(lat_coef, lon_coef, at_south, at_north):
    size, width = lat_coef.shape
    row = iota((8, width), 0)
    lat_prev = pltpu.roll(lat_coef, 1, 0)
    head = jnp.where(jnp.logical_and(row == 0, at_south), 0.0, lat_prev[:8])
    lat_prev = jnp.concatenate([head, lat_prev[8:]], axis=0)
    lon_prev = pltpu.roll(lon_coef, 1, 1)
    centre = 1.0 - lat_coef - lat_prev - lon_coef - lon_prev
    last = jnp.where(jnp.logical_and(row == 7, at_north), 0.0, lat_coef[size - 16 : size - 8])
    lat_next = jnp.concatenate([lat_coef[: size - 16], last, lat_coef[size - 8 :]], axis=0)
    return centre, lat_next, lat_prev, lon_coef, lon_prev


def diffuse_step(h, coefs):
    size, width = h.shape
    centre, lat_coef, lat_prev, lon_coef, lon_prev = coefs
    return (
        centre * h
        + lat_coef * pltpu.roll(h, size - 1, 0)
        + lat_prev * pltpu.roll(h, 1, 0)
        + lon_coef * pltpu.roll(h, width - 1, 1)
        + lon_prev * pltpu.roll(h, 1, 1)
    )


def diffuse(fields, coefs):
    for _ in range(DSTEPS):
        fields = [[diffuse_step(h, c) for h in tiles] for tiles, c in zip(fields, coefs)]
    return fields


def main_kernel(
    place_ref, field_ref, north_ref, south_ref, lat_ref, lon_ref, cnorth_ref, csouth_ref, out_ref
):
    slabs, rows, _ = lat_ref.shape
    at_south, at_north = place_ref[0] == 1, place_ref[1] == 1

    def body(step, _):
        tiles = [4 * step + i for i in range(4)]
        coefs = [
            coefs_of(
                with_rim(lat_ref[j], cnorth_ref[j], csouth_ref[j]),
                with_rim(lon_ref[j], cnorth_ref[slabs + j], csouth_ref[slabs + j]),
                at_south,
                at_north,
            )
            for j in tiles
        ]
        fields = [
            [with_rim(field_ref[i], north_ref[i], south_ref[i]) for i in (j, slabs + j)]
            for j in tiles
        ]
        for j, results in zip(tiles, diffuse(fields, coefs)):
            for m in range(2):
                out_ref[m * slabs + j] = results[m][:rows]
        return 0

    lax.fori_loop(0, slabs // 4, body, 0)


def gather_kernel(
    place_ref, flag_ref, strip_ref, cstrip_ref, east_ref, west_ref,
    main_ref, sigma_ref, slot_ref, back_ref, grid_ref, rows_ref, back_scr,
):
    slabs, rows, columns = sigma_ref.shape
    cap = slot_ref.shape[1]
    groups = slabs // 4
    at_south, at_north = place_ref[0] == 1, place_ref[1] == 1
    size = strip_ref.shape[1]
    place = iota((size, 128), 1) % SLOT
    column = iota((rows, columns), 1)
    inner = jnp.logical_and(column >= RIM, column < columns - RIM)

    def joined(strip, east, west, g):
        east = pltpu.roll(east, (8 - RIM * g) % 128, 1)
        west = pltpu.roll(west, (12 - RIM * g) % 128, 1)
        return jnp.where(place // RIM == 2, east, jnp.where(place // RIM == 3, west, strip))

    for first in range(0, groups, 4):
        tiles = range(first, first + 4)
        coefs = [
            coefs_of(
                *(
                    joined(cstrip_ref[groups * a + g], east_ref[2 + a], west_ref[2 + a], g)
                    for a in range(2)
                ),
                at_south,
                at_north,
            )
            for g in tiles
        ]
        fields = [
            [joined(strip_ref[groups * m + g], east_ref[m], west_ref[m], g) for m in range(2)]
            for g in tiles
        ]
        for g, results in zip(tiles, diffuse(fields, coefs)):
            for m in range(2):
                h = results[m][:rows]
                outer = jnp.where(place[:rows] < 8, h, pltpu.roll(h, 120, 1))
                for i in range(4):
                    j = 4 * g + i
                    edges = pltpu.roll(outer, (120 - SLOT * i) % 128, 1)
                    whole = jnp.where(inner, main_ref[m * slabs + j], edges) * sigma_ref[j]
                    grid_ref[rows * j : rows * (j + 1), columns * m : columns * (m + 1)] = whole
    grid = grid_ref[...].T.astype(BF16)
    back_scr[...] = jnp.zeros_like(back_scr)

    def body(step, _):
        k = step * RANKS_AT_ONCE
        used = halves(flag_ref, k)
        for test, first, length in branches(used, slabs):

            @pl.when(test)
            def _():
                fill_rows(rows_ref, slot_ref, k, first, length, rows)
                part_of_grid = grid[:, rows * first : rows * (first + length)]
                picked = dot(part_of_grid, rows_ref[: rows * length])
                for i in range(RANKS_AT_ONCE):
                    weight = column_weights(slot_ref, k + i, columns)
                    for m in range(2):
                        part = picked[columns * m : columns * (m + 1), 128 * i : 128 * (i + 1)]
                        at = pl.ds(cap * m + k + i, 1)
                        back_scr[at, :] = jnp.sum(part * weight, axis=0, keepdims=True)

        return 0

    lax.fori_loop(0, cap // RANKS_AT_ONCE, body, 0)
    back_ref[...] = back_scr[...].T.astype(BF16)


def unpack_kernel(
    place_ref, back_ref, recv_ref, dest_ref, rank_ref, p_ref, r_ref, var_ref, panel_ref,
    applied_ref, sums_ref,
):
    peers = back_ref.shape[0]
    cap = back_ref.shape[1] // 2
    count = p_ref.shape[1]
    lat_count = panel_ref.shape[1] // cap
    lon_count = peers // lat_count
    recv = recv_ref[...].astype(F32)[:, 3, :].astype(BF16)
    mine = iota((16, peers), 1) == iota((16, peers), 0) * lon_count + place_ref[2]
    group = dot(mine.astype(F32).astype(BF16), recv)
    corr = jnp.zeros((2, cap), F32)
    for i in range(lat_count):
        pair = jnp.concatenate([group[i : i + 1, :cap], group[i : i + 1, cap:]], axis=0)
        corr = corr + dot(pair.astype(BF16), panel_ref[:, cap * i : cap * (i + 1)], NT)
    corr = jnp.concatenate([corr, jnp.zeros((2, BLOCK - cap), F32)], axis=1)
    back = back_ref[...].astype(F32).T.astype(BF16)
    sums = [jnp.zeros((2, BLOCK), F32) for _ in range(4)]
    for start in range(0, count, BLOCK):
        at = slice(start, start + BLOCK)
        hot = (iota((peers, BLOCK), 0) == dest_ref[:, at]).astype(F32).astype(BF16)
        rank_hot = (iota((cap, BLOCK), 0) == rank_ref[:, at].astype(jnp.int32)).astype(F32)
        values = dot(back, hot)
        forward = [
            jnp.sum(values[cap * m : cap * (m + 1)] * rank_hot, axis=0, keepdims=True)
            for m in range(2)
        ]
        p = p_ref[:, at]
        r = r_ref[:, at]
        applied = jnp.concatenate(forward, axis=0) + var_ref[:, at] * p
        if start == 0:
            applied = applied + corr
        applied_ref[:, at] = applied
        for i, product in enumerate((p * applied, r * r, r * applied, applied * applied)):
            sums[i] = sums[i] + product
    lane = iota((2, 128), 1)
    row = iota((2, 128), 0)
    out = jnp.zeros((2, 128), F32)
    for i in range(4):
        total = jnp.sum(sums[i], axis=1, keepdims=True)
        out = out + jnp.where(lane == 2 * i + row, total, 0.0)
    sums_ref[...] = jnp.broadcast_to(jnp.sum(out, axis=0, keepdims=True), (peers, 128))


def update_kernel(sums_ref, applied_ref, w_ref, r_ref, p_ref, w_out, r_out, p_out):
    sums = jnp.sum(sums_ref[...], axis=0, keepdims=True)
    for m in range(2):
        at = slice(m, m + 1)
        curvature, norm_old, cross, square = (
            sums[:, 2 * i + m : 2 * i + m + 1] for i in range(4)
        )
        step = norm_old / curvature
        norm_new = norm_old - 2.0 * step * cross + step * step * square
        p = p_ref[at]
        r_next = r_ref[at] - step * applied_ref[at]
        w_out[at] = w_ref[at] + step * p
        r_out[at] = r_next
        p_out[at] = r_next + (norm_new / norm_old) * p


def shift(value, axis, steps):
    count = lax.axis_size(axis)
    return lax.ppermute(value, axis, [(i, (i + steps) % count) for i in range(count)])


def exchange(array):
    return lax.all_to_all(array, ("lat", "lon"), split_axis=0, concat_axis=0, tiled=True)


def local(
    w_obs, r_obs, p_obs, obs_dest, obs_row, obs_col, obs_level, obs_field, obs_frac, obs_var,
    corr_panel, sigma_b, coef_lat, coef_lon,
):
    lat_count = lax.axis_size("lat")
    lon_count = lax.axis_size("lon")
    peers = lat_count * lon_count
    count = p_obs.shape[1]
    cap = 2 * count // peers
    fields, levels, rows, columns = sigma_b.shape
    slabs = fields * levels
    shape = jax.ShapeDtypeStruct
    place = jnp.stack(
        [
            (lax.axis_index("lat") == 0).astype(jnp.int32),
            (lax.axis_index("lat") == lat_count - 1).astype(jnp.int32),
            lax.axis_index("lon"),
        ]
    ).astype(jnp.int32)
    smem = pl.BlockSpec(memory_space=pltpu.SMEM)
    vmem = pl.BlockSpec(memory_space=pltpu.VMEM)
    hbm = pl.BlockSpec(memory_space=pltpu.HBM)

    sigma = sigma_b.reshape(slabs, rows, columns)
    lat_coef = coef_lat.reshape(slabs, rows, columns)
    lon_coef = coef_lon.reshape(slabs, rows, columns)
    edges = lambda at: jnp.concatenate([lat_coef[:, at], lon_coef[:, at]], axis=0)
    coef_south = shift(edges(slice(rows - RIM, None)), "lat", 1)
    coef_north = shift(edges(slice(0, RIM)), "lat", -1)
    ext = rows + 2 * RIM
    groups = slabs // 4

    def strips(sources, *arrays):
        outer = shape((len(arrays) - sources, ext, 128), F32)
        return call(
            functools.partial(strip_kernel, sources),
            (shape((2 * groups, ext, 128), F32), outer, outer),
            24, 500_000_000, 4_000_000,
        )(*arrays)

    cstrip, c_east, c_west = strips(2, lat_coef, lon_coef, coef_north, coef_south)

    line = lambda a: a.reshape(1, count)
    dest = line(obs_dest)
    pair = pltpu.VMEM((2, count), F32)
    single = pltpu.VMEM((1, count), jnp.int32)
    send, rank = pl.pallas_call(
        functools.partial(pack_kernel, slabs // 2, levels, rows, columns, cap),
        out_shape=(shape((peers, 4, 128), BF16), shape((1, count), F32)),
        in_specs=[hbm] * 7,
        out_specs=(vmem, vmem),
        scratch_shapes=[pair, pair] + [single] * 5 + [pltpu.SemaphoreType.DMA((7,))],
        compiler_params=pltpu.CompilerParams(vmem_limit_bytes=56 * MIB),
        cost_estimate=pl.CostEstimate(flops=2_000_000_000, bytes_accessed=500_000, transcendentals=0),
    )(p_obs, obs_frac, dest, line(obs_row), line(obs_col), line(obs_level), line(obs_field))
    recv = exchange(send)

    width = 128 * RANKS_AT_ONCE
    field, to_north, to_south, slot, flags = call(
        scatter_kernel,
        (
            shape((2 * slabs, rows, columns), F32),
            shape((2 * slabs, RIM, columns), F32),
            shape((2 * slabs, RIM, columns), F32),
            shape((7, cap, peers), F32),
            shape((1, 128), jnp.int32),
        ),
        32, 9_000_000_000, 4_000_000,
        (
            pltpu.VMEM((slabs * rows, width), BF16),
            pltpu.VMEM((2 * columns, width), BF16),
            pltpu.VMEM((slabs * rows, 2 * columns), F32),
            pltpu.SMEM((1, 128), jnp.int32),
            pltpu.SemaphoreType.DMA,
        ),
    )(recv, sigma)
    south = shift(to_north, "lat", 1)
    north = shift(to_south, "lat", -1)
    strip, to_east, to_west = strips(1, field, north, south, c_east, c_west)
    west = shift(to_east, "lon", 1)
    east = shift(to_west, "lon", -1)

    done = pl.pallas_call(
        main_kernel,
        out_shape=shape((2 * slabs, rows, columns), F32),
        in_specs=[smem] + [vmem] * 7,
        out_specs=vmem,
        compiler_params=pltpu.CompilerParams(vmem_limit_bytes=24 * MIB),
        cost_estimate=pl.CostEstimate(flops=5_000_000_000, bytes_accessed=8_000_000, transcendentals=0),
    )(place, field, north, south, lat_coef, lon_coef, coef_north, coef_south)

    back = pl.pallas_call(
        gather_kernel,
        out_shape=shape((peers, 2 * cap), BF16),
        in_specs=[smem, smem] + [vmem] * 7,
        out_specs=vmem,
        scratch_shapes=[
            pltpu.VMEM((slabs * rows, 2 * columns), F32),
            pltpu.VMEM((slabs * rows, width), BF16),
            pltpu.VMEM((2 * cap, peers), F32),
        ],
        compiler_params=pltpu.CompilerParams(vmem_limit_bytes=36 * MIB),
        cost_estimate=pl.CostEstimate(flops=9_000_000_000, bytes_accessed=8_000_000, transcendentals=0),
    )(place, flags, strip, cstrip, east, west, done, sigma, slot)
    back = exchange(back)

    applied, sums = pl.pallas_call(
        unpack_kernel,
        out_shape=(shape((2, count), F32), shape((peers, 128), F32)),
        in_specs=[smem] + [vmem] * 8,
        out_specs=(vmem, vmem),
        compiler_params=pltpu.CompilerParams(vmem_limit_bytes=16 * MIB),
        cost_estimate=pl.CostEstimate(flops=300_000_000, bytes_accessed=500_000, transcendentals=0),
    )(place, back, recv, dest, rank, p_obs, r_obs, line(obs_var), corr_panel[0].T)
    sums = exchange(sums)
    whole = shape((2, count), F32)
    return call(update_kernel, (whole, whole, whole), 8, 100_000, 300_000)(
        sums, applied, w_obs, r_obs, p_obs
    )


def solution(mesh):
    both = ("lat", "lon")
    row = P(None, both)
    grid = P(None, None, "lat", "lon")
    in_specs = (
        row, row, row, P(both, None), P(both), P(both), P(both), P(both), row, P(both),
        P("lon", None, "lat"), grid, grid, grid,
    )
    return jax.shard_map(local, mesh=mesh, in_specs=in_specs, out_specs=(row, row, row), check_vma=False)
```

```python
import functools

import jax
import jax.numpy as jnp
from jax import lax
from jax.experimental import pallas as pl
from jax.experimental.pallas import tpu as pltpu
from jax.sharding import PartitionSpec as P

F32 = jnp.float32
BF16 = jnp.bfloat16
DSTEPS = 4
RIM = 4
SLOT = 32
NT = (((1,), (1,)), ((), ()))
NN = (((1,), (0,)), ((), ()))
BLOCK = 512
PACK_BLOCK = 512
RANKS_AT_ONCE = 8
MIB = 1024 * 1024


def dot(a, b, dims=NN):
    return lax.dot_general(a, b, dims, preferred_element_type=F32)


def iota(shape, dim):
    return lax.broadcasted_iota(jnp.int32, shape, dim)


def call(kernel, out_shape, vmem, flops, moved, scratch=()):
    return pl.pallas_call(
        kernel,
        out_shape=out_shape,
        scratch_shapes=list(scratch),
        compiler_params=pltpu.CompilerParams(vmem_limit_bytes=vmem * MIB),
        cost_estimate=pl.CostEstimate(flops=flops, bytes_accessed=moved, transcendentals=0),
    )


def pack_kernel(
    half, levels, rows, columns, cap,
    p_hbm, frac_hbm, dest_hbm, row_hbm, col_hbm, level_hbm, field_hbm, send_ref, rank_ref,
    p_ref, frac_ref, dest_ref, row_ref, col_ref, level_ref, field_ref, sems,
):
    sources = (p_hbm, frac_hbm, dest_hbm, row_hbm, col_hbm, level_hbm, field_hbm)
    targets = (p_ref, frac_ref, dest_ref, row_ref, col_ref, level_ref, field_ref)
    copies = [
        pltpu.make_async_copy(source, target, sems.at[i])
        for i, (source, target) in enumerate(zip(sources, targets))
    ]
    for copy in copies:
        copy.start()
    for copy in copies:
        copy.wait()
    peers = send_ref.shape[0]
    count = p_ref.shape[1]
    part = PACK_BLOCK // 2
    order = (iota((part, part), 0) < iota((part, part), 1)).astype(BF16)
    before = jnp.zeros((2 * peers, 1), F32)
    total = jnp.zeros((peers, 6 * cap), F32)

    def keys(start):
        at = slice(start, start + PACK_BLOCK)
        slab = field_ref[:, at] * levels + level_ref[:, at]
        upper = slab >= half
        key = jnp.where(upper, peers, 0) + dest_ref[:, at]
        hot = (iota((2 * peers, PACK_BLOCK), 0) == key).astype(F32)
        hot16 = hot.astype(BF16)
        counts = (dot(hot16[:, :part], order), dot(hot16[:, part:], order))
        sums = [jnp.sum(h, axis=1, keepdims=True) for h in (hot[:, :part], hot[:, part:])]
        return slab, upper, hot, counts, sums

    ready = keys(0)
    for start in range(0, count, PACK_BLOCK):
        at = slice(start, start + PACK_BLOCK)
        slab, upper, hot, counts, sums = ready
        if start + PACK_BLOCK < count:
            ready = keys(start + PACK_BLOCK)
        middle = before + sums[0]
        counts = jnp.concatenate([counts[0] + before, counts[1] + middle], axis=1)
        rank = jnp.sum(hot * counts, axis=0, keepdims=True)
        before = middle + sums[1]
        rank = jnp.where(upper, cap - 1.0 - rank, rank)
        hot16 = (hot[:peers] + hot[peers:]).astype(BF16)
        rank_ref[:, at] = rank
        rank_hot = (iota((cap, PACK_BLOCK), 0) == rank.astype(jnp.int32)).astype(F32)
        cell = (slab * rows + row_ref[:, at]) * columns + col_ref[:, at]
        high = cell >> 9
        high = (jnp.where(upper, high + 1, high) - 256).astype(F32)
        low = ((cell & 511) - 256).astype(F32)
        frac = jnp.floor(frac_ref[:, at] * 256.0 + 0.5) * (1.0 / 256.0)
        p = p_ref[:, at]
        values = (p[0:1], p[1:2], frac[0:1], frac[1:2], high, low)
        payload = jnp.concatenate([(rank_hot * v).astype(BF16) for v in values], axis=0)
        total = total + dot(hot16, payload, NT)
    lane = iota((8, 128), 1)
    first = jnp.broadcast_to(p_ref[0:1, 0:128], (8, 128))
    second = pltpu.roll(jnp.broadcast_to(p_ref[1:2, 0:128], (8, 128)), 64, 1)
    corr = jnp.where(lane < 64, first, second)[0:1]
    pieces = [total[:, 128 * i : 128 * (i + 1)] for i in range(3)]
    pieces.append(jnp.broadcast_to(corr, (peers, 128)))
    send_ref[...] = jnp.stack(pieces, axis=1).astype(BF16)


def fill_rows(rows_ref, slot_ref, k, first, slabs, rows):
    for i in range(RANKS_AT_ONCE):
        lat_frac = slot_ref[2, pl.ds(k + i, 1), :]
        slab = slot_ref[4, pl.ds(k + i, 1), :]
        row = slot_ref[5, pl.ds(k + i, 1), :].astype(jnp.int32)
        index = iota((rows, 128), 0)
        weight = jnp.where(
            index == row, 1.0 - lat_frac, jnp.where(index == row + 1, lat_frac, 0.0)
        ).astype(BF16)
        none = jnp.zeros((rows, 128), BF16)
        slab = jnp.broadcast_to(slab, (rows, 128)).astype(BF16)
        for j in range(slabs):
            at = slice(rows * j, rows * (j + 1))
            rows_ref[at, 128 * i : 128 * (i + 1)] = jnp.where(slab == first + j, weight, none)


def halves(flag_ref, k):
    code = flag_ref[0, k]
    for i in range(1, RANKS_AT_ONCE):
        code = code | flag_ref[0, k + i]
    return (code & 1) != 0, (code & 2) != 0


def branches(used, slabs):
    lower, upper = used
    half = slabs // 2
    return (
        (jnp.logical_and(lower, upper), 0, slabs),
        (jnp.logical_and(lower, jnp.logical_not(upper)), 0, half),
        (jnp.logical_and(upper, jnp.logical_not(lower)), half, half),
    )


def column_weights(slot_ref, k, columns):
    lon_frac = slot_ref[3, pl.ds(k, 1), :]
    col = slot_ref[6, pl.ds(k, 1), :].astype(jnp.int32)
    index = iota((columns, 128), 0)
    return jnp.where(index == col, 1.0 - lon_frac, jnp.where(index == col + 1, lon_frac, 0.0))


def scatter_kernel(
    recv_ref, sigma_ref, field_ref, north_ref, south_ref, slot_ref, flag_ref,
    rows_ref, cols_ref, acc_ref, code_ref, north_f32, south_f32, sem,
):
    slabs, rows, columns = sigma_ref.shape
    cap = slot_ref.shape[1]
    recv = recv_ref[...].astype(F32)
    cells = recv[:, 2, :]
    lower = (jnp.min(cells, axis=0, keepdims=True) < 0.0).astype(jnp.int32)
    upper = (jnp.max(cells, axis=0, keepdims=True) > 0.0).astype(jnp.int32)
    flag_ref[...] = lower + 2 * upper
    copy = pltpu.make_async_copy(flag_ref, code_ref, sem)
    copy.start()
    parts = [recv[:, i, :].T for i in range(3)]
    slot_ref[0] = parts[0][:cap]
    slot_ref[1] = parts[0][cap:]
    slot_ref[2] = parts[1][:cap]
    slot_ref[3] = parts[1][cap:]
    high = parts[2][:cap].astype(jnp.int32)
    high = jnp.where(high > 0, high - 1, high) + 256
    low = parts[2][cap:].astype(jnp.int32) + 256
    cell = high * 512 + low
    slot_ref[4] = (cell >> 13).astype(F32)
    slot_ref[5] = ((cell >> 7) & 63).astype(F32)
    slot_ref[6] = (cell & 127).astype(F32)
    acc_ref[...] = jnp.zeros_like(acc_ref)
    copy.wait()

    def body(step, _):
        k = step * RANKS_AT_ONCE
        used = halves(code_ref, k)

        for test, first, length in branches(used, slabs):

            @pl.when(test)
            def _():
                for i in range(RANKS_AT_ONCE):
                    weight = column_weights(slot_ref, k + i, columns)
                    for m in range(2):
                        p = slot_ref[m, pl.ds(k + i, 1), :]
                        cols_ref[columns * m : columns * (m + 1), 128 * i : 128 * (i + 1)] = (
                            weight * p
                        ).astype(BF16)
                fill_rows(rows_ref, slot_ref, k, first, length, rows)
                at = slice(rows * first, rows * (first + length))
                acc_ref[at] += dot(rows_ref[: rows * length], cols_ref[...], NT)

        return 0

    lax.fori_loop(0, cap // RANKS_AT_ONCE, body, 0)
    for j in range(slabs):
        for m in range(2):
            part = acc_ref[rows * j : rows * (j + 1), columns * m : columns * (m + 1)]
            part = part * sigma_ref[j]
            field_ref[m * slabs + j] = part
            north_f32[m * slabs + j] = part[rows - RIM :]
            south_f32[m * slabs + j] = part[:RIM]
    north_ref[...] = north_f32[...].astype(BF16)
    south_ref[...] = south_f32[...].astype(BF16)


def fill_rim(rim_ref, north_ref, south_ref):
    rim_ref[:, :RIM] = north_ref[...].astype(F32)
    rim_ref[:, RIM:] = south_ref[...].astype(F32)


def with_rim(main, rim):
    return jnp.concatenate([main, rim], axis=0)


def strip_kernel(sources, *refs):
    *refs, rim_ref = refs
    inputs, outputs = refs[: sources + 2], refs[sources + 2 :]
    *inputs, north_ref, south_ref = inputs
    fill_rim(rim_ref, north_ref, south_ref)
    *more, strip_ref, east_ref, west_ref = outputs
    size = strip_ref.shape[1]
    lane = iota((size, 128), 1)
    place = lane % SLOT
    slabs = north_ref.shape[0] // 2
    east = [jnp.zeros((size, 128), F32)] * 2
    west = [jnp.zeros((size, 128), F32)] * 2
    for g in range(slabs // 4):
        for a in range(2):
            ref, first = (inputs[0], slabs * a) if sources == 1 else (inputs[a], 0)
            outer = jnp.zeros((size, 128), F32)
            for i in range(4):
                j = 4 * g + i
                x = with_rim(ref[first + j], rim_ref[slabs * a + j])
                outer = jnp.where(lane // SLOT == i, pltpu.roll(x, SLOT * i + 8, 1), outer)
            strip = jnp.where(place < 8, outer, pltpu.roll(outer, 8, 1))
            inside = jnp.logical_or(place < 8, jnp.logical_and(place >= 16, place < 24))
            strip_ref[slabs // 4 * a + g] = jnp.where(inside, strip, 0.0)
            mine = place // RIM == g
            east[a] = jnp.where(mine, pltpu.roll(outer, (RIM * g - 4) % 128, 1), east[a])
            west[a] = jnp.where(mine, pltpu.roll(outer, (RIM * g - 8) % 128, 1), west[a])
    for a in range(2):
        east_ref[a] = east[a]
        west_ref[a] = west[a]
    if more:
        east_ref[2:] = more[0][...]
        west_ref[2:] = more[1][...]


def coefs_of(lat_coef, lon_coef, at_south, at_north):
    size, width = lat_coef.shape
    row = iota((8, width), 0)
    lat_prev = pltpu.roll(lat_coef, 1, 0)
    head = jnp.where(jnp.logical_and(row == 0, at_south), 0.0, lat_prev[:8])
    lat_prev = jnp.concatenate([head, lat_prev[8:]], axis=0)
    lon_prev = pltpu.roll(lon_coef, 1, 1)
    centre = 1.0 - lat_coef - lat_prev - lon_coef - lon_prev
    last = jnp.where(jnp.logical_and(row == 7, at_north), 0.0, lat_coef[size - 16 : size - 8])
    lat_next = jnp.concatenate([lat_coef[: size - 16], last, lat_coef[size - 8 :]], axis=0)
    return centre, lat_next, lat_prev, lon_coef, lon_prev


def diffuse_step(h, coefs):
    size, width = h.shape
    centre, lat_coef, lat_prev, lon_coef, lon_prev = coefs
    return (
        centre * h
        + lat_coef * pltpu.roll(h, size - 1, 0)
        + lat_prev * pltpu.roll(h, 1, 0)
        + lon_coef * pltpu.roll(h, width - 1, 1)
        + lon_prev * pltpu.roll(h, 1, 1)
    )


def diffuse(fields, coefs):
    for _ in range(DSTEPS):
        fields = [[diffuse_step(h, c) for h in tiles] for tiles, c in zip(fields, coefs)]
    return fields


def main_kernel(
    place_ref, field_ref, north_ref, south_ref, lat_ref, lon_ref, cnorth_ref, csouth_ref, out_ref,
    rim_ref, crim_ref,
):
    fill_rim(rim_ref, north_ref, south_ref)
    fill_rim(crim_ref, cnorth_ref, csouth_ref)
    slabs, rows, _ = lat_ref.shape
    at_south, at_north = place_ref[0] == 1, place_ref[1] == 1

    def body(step, _):
        tiles = [4 * step + i for i in range(4)]
        coefs = [
            coefs_of(
                with_rim(lat_ref[j], crim_ref[j]),
                with_rim(lon_ref[j], crim_ref[slabs + j]),
                at_south,
                at_north,
            )
            for j in tiles
        ]
        fields = [
            [with_rim(field_ref[i], rim_ref[i]) for i in (j, slabs + j)]
            for j in tiles
        ]
        for j, results in zip(tiles, diffuse(fields, coefs)):
            for m in range(2):
                out_ref[m * slabs + j] = results[m][:rows]
        return 0

    lax.fori_loop(0, slabs // 4, body, 0)


def gather_kernel(
    place_ref, flag_ref, strip_ref, cstrip_ref, east_ref, west_ref,
    main_ref, sigma_ref, slot_ref, back_ref, grid_ref, rows_ref, back_scr,
):
    slabs, rows, columns = sigma_ref.shape
    cap = slot_ref.shape[1]
    groups = slabs // 4
    at_south, at_north = place_ref[0] == 1, place_ref[1] == 1
    size = strip_ref.shape[1]
    place = iota((size, 128), 1) % SLOT
    column = iota((rows, columns), 1)
    inner = jnp.logical_and(column >= RIM, column < columns - RIM)

    def joined(strip, east, west, g):
        east = pltpu.roll(east, (8 - RIM * g) % 128, 1)
        west = pltpu.roll(west, (12 - RIM * g) % 128, 1)
        return jnp.where(place // RIM == 2, east, jnp.where(place // RIM == 3, west, strip))

    for first in range(0, groups, 4):
        tiles = range(first, first + 4)
        coefs = [
            coefs_of(
                *(
                    joined(cstrip_ref[groups * a + g], east_ref[2 + a], west_ref[2 + a], g)
                    for a in range(2)
                ),
                at_south,
                at_north,
            )
            for g in tiles
        ]
        fields = [
            [joined(strip_ref[groups * m + g], east_ref[m], west_ref[m], g) for m in range(2)]
            for g in tiles
        ]
        for g, results in zip(tiles, diffuse(fields, coefs)):
            for m in range(2):
                h = results[m][:rows]
                outer = jnp.where(place[:rows] < 8, h, pltpu.roll(h, 120, 1))
                for i in range(4):
                    j = 4 * g + i
                    edges = pltpu.roll(outer, (120 - SLOT * i) % 128, 1)
                    whole = jnp.where(inner, main_ref[m * slabs + j], edges) * sigma_ref[j]
                    grid_ref[rows * j : rows * (j + 1), columns * m : columns * (m + 1)] = whole.astype(BF16)
    grid = grid_ref[...].T
    back_scr[...] = jnp.zeros_like(back_scr)

    def body(step, _):
        k = step * RANKS_AT_ONCE
        used = halves(flag_ref, k)
        for test, first, length in branches(used, slabs):

            @pl.when(test)
            def _():
                fill_rows(rows_ref, slot_ref, k, first, length, rows)
                part_of_grid = grid[:, rows * first : rows * (first + length)]
                picked = dot(part_of_grid, rows_ref[: rows * length])
                for i in range(RANKS_AT_ONCE):
                    weight = column_weights(slot_ref, k + i, columns)
                    for m in range(2):
                        part = picked[columns * m : columns * (m + 1), 128 * i : 128 * (i + 1)]
                        at = pl.ds(cap * m + k + i, 1)
                        back_scr[at, :] = jnp.sum(part * weight, axis=0, keepdims=True)

        return 0

    lax.fori_loop(0, cap // RANKS_AT_ONCE, body, 0)
    back_ref[...] = back_scr[...].T.astype(BF16)


def unpack_kernel(
    place_ref, back_ref, recv_ref, dest_ref, rank_ref, p_ref, r_ref, var_ref, panel_ref,
    applied_ref, sums_ref,
):
    peers = back_ref.shape[0]
    cap = back_ref.shape[1] // 2
    count = p_ref.shape[1]
    lat_count = panel_ref.shape[1] // cap
    lon_count = peers // lat_count
    recv = recv_ref[...].astype(F32)[:, 3, :].astype(BF16)
    mine = iota((16, peers), 1) == iota((16, peers), 0) * lon_count + place_ref[2]
    group = dot(mine.astype(F32).astype(BF16), recv)
    corr = jnp.zeros((2, cap), F32)
    for i in range(lat_count):
        pair = jnp.concatenate([group[i : i + 1, :cap], group[i : i + 1, cap:]], axis=0)
        corr = corr + dot(pair.astype(BF16), panel_ref[:, cap * i : cap * (i + 1)], NT)
    corr = jnp.concatenate([corr, jnp.zeros((2, BLOCK - cap), F32)], axis=1)
    back = back_ref[...].astype(F32).T.astype(BF16)
    sums = [jnp.zeros((2, BLOCK), F32) for _ in range(4)]
    for start in range(0, count, BLOCK):
        at = slice(start, start + BLOCK)
        hot = (iota((peers, BLOCK), 0) == dest_ref[:, at]).astype(F32).astype(BF16)
        rank_hot = (iota((cap, BLOCK), 0) == rank_ref[:, at].astype(jnp.int32)).astype(F32)
        values = dot(back, hot)
        forward = [
            jnp.sum(values[cap * m : cap * (m + 1)] * rank_hot, axis=0, keepdims=True)
            for m in range(2)
        ]
        p = p_ref[:, at]
        r = r_ref[:, at]
        applied = jnp.concatenate(forward, axis=0) + var_ref[:, at] * p
        if start == 0:
            applied = applied + corr
        applied_ref[:, at] = applied
        for i, product in enumerate((p * applied, r * r, r * applied, applied * applied)):
            sums[i] = sums[i] + product
    lane = iota((2, 128), 1)
    row = iota((2, 128), 0)
    out = jnp.zeros((2, 128), F32)
    for i in range(4):
        total = jnp.sum(sums[i], axis=1, keepdims=True)
        out = out + jnp.where(lane == 2 * i + row, total, 0.0)
    sums_ref[...] = jnp.broadcast_to(jnp.sum(out, axis=0, keepdims=True), (peers, 128))


def update_kernel(sums_ref, applied_ref, w_ref, r_ref, p_ref, w_out, r_out, p_out):
    sums = jnp.sum(sums_ref[...], axis=0, keepdims=True)
    for m in range(2):
        at = slice(m, m + 1)
        curvature, norm_old, cross, square = (
            sums[:, 2 * i + m : 2 * i + m + 1] for i in range(4)
        )
        step = norm_old / curvature
        norm_new = norm_old - 2.0 * step * cross + step * step * square
        p = p_ref[at]
        r_next = r_ref[at] - step * applied_ref[at]
        w_out[at] = w_ref[at] + step * p
        r_out[at] = r_next
        p_out[at] = r_next + (norm_new / norm_old) * p


def shift(value, axis, steps):
    count = lax.axis_size(axis)
    return lax.ppermute(value, axis, [(i, (i + steps) % count) for i in range(count)])


def exchange(array):
    return lax.all_to_all(array, ("lat", "lon"), split_axis=0, concat_axis=0, tiled=True)


def local(
    w_obs, r_obs, p_obs, obs_dest, obs_row, obs_col, obs_level, obs_field, obs_frac, obs_var,
    corr_panel, sigma_b, coef_lat, coef_lon,
):
    lat_count = lax.axis_size("lat")
    lon_count = lax.axis_size("lon")
    peers = lat_count * lon_count
    count = p_obs.shape[1]
    cap = 2 * count // peers
    fields, levels, rows, columns = sigma_b.shape
    slabs = fields * levels
    shape = jax.ShapeDtypeStruct
    place = jnp.stack(
        [
            (lax.axis_index("lat") == 0).astype(jnp.int32),
            (lax.axis_index("lat") == lat_count - 1).astype(jnp.int32),
            lax.axis_index("lon"),
        ]
    ).astype(jnp.int32)
    smem = pl.BlockSpec(memory_space=pltpu.SMEM)
    vmem = pl.BlockSpec(memory_space=pltpu.VMEM)
    hbm = pl.BlockSpec(memory_space=pltpu.HBM)

    sigma = sigma_b.reshape(slabs, rows, columns)
    lat_coef = coef_lat.reshape(slabs, rows, columns)
    lon_coef = coef_lon.reshape(slabs, rows, columns)
    edges = lambda at: jnp.concatenate([lat_coef[:, at], lon_coef[:, at]], axis=0).astype(BF16)
    rim = pltpu.VMEM((2 * slabs, RIM, columns), F32)
    both_rims = pltpu.VMEM((2 * slabs, 2 * RIM, columns), F32)
    coef_south = shift(edges(slice(rows - RIM, None)), "lat", 1)
    coef_north = shift(edges(slice(0, RIM)), "lat", -1)
    ext = rows + 2 * RIM
    groups = slabs // 4

    def strips(sources, *arrays):
        outer = shape((len(arrays) - sources, ext, 128), F32)
        return call(
            functools.partial(strip_kernel, sources),
            (shape((2 * groups, ext, 128), F32), outer, outer),
            24, 500_000_000, 4_000_000,
            (both_rims,),
        )(*arrays)

    cstrip, c_east, c_west = strips(2, lat_coef, lon_coef, coef_north, coef_south)

    line = lambda a: a.reshape(1, count)
    dest = line(obs_dest)
    pair = pltpu.VMEM((2, count), F32)
    single = pltpu.VMEM((1, count), jnp.int32)
    send, rank = pl.pallas_call(
        functools.partial(pack_kernel, slabs // 2, levels, rows, columns, cap),
        out_shape=(shape((peers, 4, 128), BF16), shape((1, count), F32)),
        in_specs=[hbm] * 7,
        out_specs=(vmem, vmem),
        scratch_shapes=[pair, pair] + [single] * 5 + [pltpu.SemaphoreType.DMA((7,))],
        compiler_params=pltpu.CompilerParams(vmem_limit_bytes=56 * MIB),
        cost_estimate=pl.CostEstimate(flops=2_000_000_000, bytes_accessed=500_000, transcendentals=0),
    )(p_obs, obs_frac, dest, line(obs_row), line(obs_col), line(obs_level), line(obs_field))
    recv = exchange(send)

    width = 128 * RANKS_AT_ONCE
    field, to_north, to_south, slot, flags = call(
        scatter_kernel,
        (
            shape((2 * slabs, rows, columns), F32),
            shape((2 * slabs, RIM, columns), BF16),
            shape((2 * slabs, RIM, columns), BF16),
            shape((7, cap, peers), F32),
            shape((1, 128), jnp.int32),
        ),
        32, 9_000_000_000, 4_000_000,
        (
            pltpu.VMEM((slabs * rows, width), BF16),
            pltpu.VMEM((2 * columns, width), BF16),
            pltpu.VMEM((slabs * rows, 2 * columns), F32),
            pltpu.SMEM((1, 128), jnp.int32),
            rim,
            rim,
            pltpu.SemaphoreType.DMA,
        ),
    )(recv, sigma)
    south = shift(to_north, "lat", 1)
    north = shift(to_south, "lat", -1)
    strip, to_east, to_west = strips(1, field, north, south, c_east, c_west)
    west = shift(to_east, "lon", 1)
    east = shift(to_west, "lon", -1)

    done = pl.pallas_call(
        main_kernel,
        out_shape=shape((2 * slabs, rows, columns), F32),
        in_specs=[smem] + [vmem] * 7,
        out_specs=vmem,
        scratch_shapes=[both_rims] * 2,
        compiler_params=pltpu.CompilerParams(vmem_limit_bytes=24 * MIB),
        cost_estimate=pl.CostEstimate(flops=5_000_000_000, bytes_accessed=8_000_000, transcendentals=0),
    )(place, field, north, south, lat_coef, lon_coef, coef_north, coef_south)

    back = pl.pallas_call(
        gather_kernel,
        out_shape=shape((peers, 2 * cap), BF16),
        in_specs=[smem, smem] + [vmem] * 7,
        out_specs=vmem,
        scratch_shapes=[
            pltpu.VMEM((slabs * rows, 2 * columns), BF16),
            pltpu.VMEM((slabs * rows, width), BF16),
            pltpu.VMEM((2 * cap, peers), F32),
        ],
        compiler_params=pltpu.CompilerParams(vmem_limit_bytes=36 * MIB),
        cost_estimate=pl.CostEstimate(flops=9_000_000_000, bytes_accessed=8_000_000, transcendentals=0),
    )(place, flags, strip, cstrip, east, west, done, sigma, slot)
    back = exchange(back)

    applied, sums = pl.pallas_call(
        unpack_kernel,
        out_shape=(shape((2, count), F32), shape((peers, 128), F32)),
        in_specs=[smem] + [vmem] * 8,
        out_specs=(vmem, vmem),
        compiler_params=pltpu.CompilerParams(vmem_limit_bytes=16 * MIB),
        cost_estimate=pl.CostEstimate(flops=300_000_000, bytes_accessed=500_000, transcendentals=0),
    )(place, back, recv, dest, rank, p_obs, r_obs, line(obs_var), corr_panel[0].T)
    sums = exchange(sums)
    whole = shape((2, count), F32)
    return call(update_kernel, (whole, whole, whole), 8, 100_000, 300_000)(
        sums, applied, w_obs, r_obs, p_obs
    )


def solution(mesh):
    both = ("lat", "lon")
    row = P(None, both)
    grid = P(None, None, "lat", "lon")
    in_specs = (
        row, row, row, P(both, None), P(both), P(both), P(both), P(both), row, P(both),
        P("lon", None, "lat"), grid, grid, grid,
    )
    return jax.shard_map(local, mesh=mesh, in_specs=in_specs, out_specs=(row, row, row), check_vma=False)
```

```python
import functools

import jax
import jax.numpy as jnp
from jax import lax
from jax.experimental import pallas as pl
from jax.experimental.pallas import tpu as pltpu
from jax.sharding import PartitionSpec as P

F32 = jnp.float32
BF16 = jnp.bfloat16
DSTEPS = 4
RIM = 4
SLOT = 32
NT = (((1,), (1,)), ((), ()))
NN = (((1,), (0,)), ((), ()))
BLOCK = 512
PACK_BLOCK = 512
RANKS_AT_ONCE = 16
MIB = 1024 * 1024


def dot(a, b, dims=NN):
    return lax.dot_general(a, b, dims, preferred_element_type=F32)


def iota(shape, dim):
    return lax.broadcasted_iota(jnp.int32, shape, dim)


def call(kernel, out_shape, vmem, flops, moved, scratch=()):
    return pl.pallas_call(
        kernel,
        out_shape=out_shape,
        scratch_shapes=list(scratch),
        compiler_params=pltpu.CompilerParams(vmem_limit_bytes=vmem * MIB),
        cost_estimate=pl.CostEstimate(flops=flops, bytes_accessed=moved, transcendentals=0),
    )


def pack_kernel(
    half, levels, rows, columns, cap,
    p_hbm, frac_hbm, dest_hbm, row_hbm, col_hbm, level_hbm, field_hbm, send_ref, rank_ref,
    p_ref, frac_ref, dest_ref, row_ref, col_ref, level_ref, field_ref, sems,
):
    sources = (p_hbm, frac_hbm, dest_hbm, row_hbm, col_hbm, level_hbm, field_hbm)
    targets = (p_ref, frac_ref, dest_ref, row_ref, col_ref, level_ref, field_ref)
    copies = [
        pltpu.make_async_copy(source, target, sems.at[i])
        for i, (source, target) in enumerate(zip(sources, targets))
    ]
    for copy in copies:
        copy.start()
    for copy in copies:
        copy.wait()
    peers = send_ref.shape[0]
    count = p_ref.shape[1]
    part = PACK_BLOCK // 2
    order = (iota((part, part), 0) < iota((part, part), 1)).astype(BF16)
    before = jnp.zeros((2 * peers, 1), F32)
    total = jnp.zeros((peers, 6 * cap), F32)

    def keys(start):
        at = slice(start, start + PACK_BLOCK)
        slab = field_ref[:, at] * levels + level_ref[:, at]
        upper = slab >= half
        key = jnp.where(upper, peers, 0) + dest_ref[:, at]
        hot = (iota((2 * peers, PACK_BLOCK), 0) == key).astype(F32)
        hot16 = hot.astype(BF16)
        counts = (dot(hot16[:, :part], order), dot(hot16[:, part:], order))
        sums = [jnp.sum(h, axis=1, keepdims=True) for h in (hot[:, :part], hot[:, part:])]
        return slab, upper, hot, counts, sums

    ready = keys(0)
    for start in range(0, count, PACK_BLOCK):
        at = slice(start, start + PACK_BLOCK)
        slab, upper, hot, counts, sums = ready
        if start + PACK_BLOCK < count:
            ready = keys(start + PACK_BLOCK)
        middle = before + sums[0]
        counts = jnp.concatenate([counts[0] + before, counts[1] + middle], axis=1)
        rank = jnp.sum(hot * counts, axis=0, keepdims=True)
        before = middle + sums[1]
        rank = jnp.where(upper, cap - 1.0 - rank, rank)
        hot16 = (hot[:peers] + hot[peers:]).astype(BF16)
        rank_ref[:, at] = rank
        rank_hot = (iota((cap, PACK_BLOCK), 0) == rank.astype(jnp.int32)).astype(F32)
        cell = (slab * rows + row_ref[:, at]) * columns + col_ref[:, at]
        high = cell >> 9
        high = (jnp.where(upper, high + 1, high) - 256).astype(F32)
        low = ((cell & 511) - 256).astype(F32)
        frac = jnp.floor(frac_ref[:, at] * 256.0 + 0.5) * (1.0 / 256.0)
        p = p_ref[:, at]
        values = (p[0:1], p[1:2], frac[0:1], frac[1:2], high, low)
        payload = jnp.concatenate([(rank_hot * v).astype(BF16) for v in values], axis=0)
        total = total + dot(hot16, payload, NT)
    lane = iota((8, 128), 1)
    first = jnp.broadcast_to(p_ref[0:1, 0:128], (8, 128))
    second = pltpu.roll(jnp.broadcast_to(p_ref[1:2, 0:128], (8, 128)), 64, 1)
    corr = jnp.where(lane < 64, first, second)[0:1]
    pieces = [total[:, 128 * i : 128 * (i + 1)] for i in range(3)]
    pieces.append(jnp.broadcast_to(corr, (peers, 128)))
    send_ref[...] = jnp.stack(pieces, axis=1).astype(BF16)


def fill_rows(rows_ref, slot_ref, k, first, slabs, rows):
    for i in range(RANKS_AT_ONCE):
        lat_frac = slot_ref[2, pl.ds(k + i, 1), :]
        slab = slot_ref[4, pl.ds(k + i, 1), :]
        row = slot_ref[5, pl.ds(k + i, 1), :].astype(jnp.int32)
        index = iota((rows, 128), 0)
        weight = jnp.where(
            index == row, 1.0 - lat_frac, jnp.where(index == row + 1, lat_frac, 0.0)
        ).astype(BF16)
        none = jnp.zeros((rows, 128), BF16)
        slab = jnp.broadcast_to(slab, (rows, 128)).astype(BF16)
        for j in range(slabs):
            at = slice(rows * j, rows * (j + 1))
            rows_ref[at, 128 * i : 128 * (i + 1)] = jnp.where(slab == first + j, weight, none)


def halves(flag_ref, k):
    code = flag_ref[0, k]
    for i in range(1, RANKS_AT_ONCE):
        code = code | flag_ref[0, k + i]
    return (code & 1) != 0, (code & 2) != 0


def branches(used, slabs):
    lower, upper = used
    half = slabs // 2
    return (
        (jnp.logical_and(lower, upper), 0, slabs),
        (jnp.logical_and(lower, jnp.logical_not(upper)), 0, half),
        (jnp.logical_and(upper, jnp.logical_not(lower)), half, half),
    )


def column_weights(slot_ref, k, columns):
    lon_frac = slot_ref[3, pl.ds(k, 1), :]
    col = slot_ref[6, pl.ds(k, 1), :].astype(jnp.int32)
    index = iota((columns, 128), 0)
    return jnp.where(index == col, 1.0 - lon_frac, jnp.where(index == col + 1, lon_frac, 0.0))


def scatter_kernel(
    recv_ref, sigma_ref, field_ref, north_ref, south_ref, slot_ref, flag_ref,
    rows_ref, cols_ref, acc_ref, code_ref, north_f32, south_f32, sem,
):
    slabs, rows, columns = sigma_ref.shape
    cap = slot_ref.shape[1]
    recv = recv_ref[...].astype(F32)
    cells = recv[:, 2, :]
    lower = (jnp.min(cells, axis=0, keepdims=True) < 0.0).astype(jnp.int32)
    upper = (jnp.max(cells, axis=0, keepdims=True) > 0.0).astype(jnp.int32)
    flag_ref[...] = lower + 2 * upper
    copy = pltpu.make_async_copy(flag_ref, code_ref, sem)
    copy.start()
    parts = [recv[:, i, :].T for i in range(3)]
    slot_ref[0] = parts[0][:cap]
    slot_ref[1] = parts[0][cap:]
    slot_ref[2] = parts[1][:cap]
    slot_ref[3] = parts[1][cap:]
    high = parts[2][:cap].astype(jnp.int32)
    high = jnp.where(high > 0, high - 1, high) + 256
    low = parts[2][cap:].astype(jnp.int32) + 256
    cell = high * 512 + low
    slot_ref[4] = (cell >> 13).astype(F32)
    slot_ref[5] = ((cell >> 7) & 63).astype(F32)
    slot_ref[6] = (cell & 127).astype(F32)
    acc_ref[...] = jnp.zeros_like(acc_ref)
    copy.wait()

    def body(step, _):
        k = step * RANKS_AT_ONCE
        used = halves(code_ref, k)

        for test, first, length in branches(used, slabs):

            @pl.when(test)
            def _():
                for i in range(RANKS_AT_ONCE):
                    weight = column_weights(slot_ref, k + i, columns)
                    for m in range(2):
                        p = slot_ref[m, pl.ds(k + i, 1), :]
                        cols_ref[columns * m : columns * (m + 1), 128 * i : 128 * (i + 1)] = (
                            weight * p
                        ).astype(BF16)
                fill_rows(rows_ref, slot_ref, k, first, length, rows)
                at = slice(rows * first, rows * (first + length))
                acc_ref[at] += dot(rows_ref[: rows * length], cols_ref[...], NT)

        return 0

    lax.fori_loop(0, cap // RANKS_AT_ONCE, body, 0)
    for j in range(slabs):
        for m in range(2):
            part = acc_ref[rows * j : rows * (j + 1), columns * m : columns * (m + 1)]
            part = part * sigma_ref[j]
            field_ref[m * slabs + j] = part
            north_f32[m * slabs + j] = part[rows - RIM :]
            south_f32[m * slabs + j] = part[:RIM]
    north_ref[...] = north_f32[...].astype(BF16)
    south_ref[...] = south_f32[...].astype(BF16)


def fill_rim(rim_ref, north_ref, south_ref):
    rim_ref[:, :RIM] = north_ref[...].astype(F32)
    rim_ref[:, RIM:] = south_ref[...].astype(F32)


def with_rim(main, rim):
    return jnp.concatenate([main, rim], axis=0)


def strip_kernel(sources, *refs):
    *refs, rim_ref = refs
    inputs, outputs = refs[: sources + 2], refs[sources + 2 :]
    *inputs, north_ref, south_ref = inputs
    fill_rim(rim_ref, north_ref, south_ref)
    *more, strip_ref, east_ref, west_ref = outputs
    size = strip_ref.shape[1]
    lane = iota((size, 128), 1)
    place = lane % SLOT
    slabs = north_ref.shape[0] // 2
    east = [jnp.zeros((size, 128), F32)] * 2
    west = [jnp.zeros((size, 128), F32)] * 2
    for g in range(slabs // 4):
        for a in range(2):
            ref, first = (inputs[0], slabs * a) if sources == 1 else (inputs[a], 0)
            outer = jnp.zeros((size, 128), F32)
            for i in range(4):
                j = 4 * g + i
                x = with_rim(ref[first + j], rim_ref[slabs * a + j])
                outer = jnp.where(lane // SLOT == i, pltpu.roll(x, SLOT * i + 8, 1), outer)
            strip = jnp.where(place < 8, outer, pltpu.roll(outer, 8, 1))
            inside = jnp.logical_or(place < 8, jnp.logical_and(place >= 16, place < 24))
            strip_ref[slabs // 4 * a + g] = jnp.where(inside, strip, 0.0)
            mine = place // RIM == g
            east[a] = jnp.where(mine, pltpu.roll(outer, (RIM * g - 4) % 128, 1), east[a])
            west[a] = jnp.where(mine, pltpu.roll(outer, (RIM * g - 8) % 128, 1), west[a])
    for a in range(2):
        east_ref[a] = east[a]
        west_ref[a] = west[a]
    if more:
        east_ref[2:] = more[0][...]
        west_ref[2:] = more[1][...]


def coefs_of(lat_coef, lon_coef, at_south, at_north):
    size, width = lat_coef.shape
    row = iota((8, width), 0)
    lat_prev = pltpu.roll(lat_coef, 1, 0)
    head = jnp.where(jnp.logical_and(row == 0, at_south), 0.0, lat_prev[:8])
    lat_prev = jnp.concatenate([head, lat_prev[8:]], axis=0)
    lon_prev = pltpu.roll(lon_coef, 1, 1)
    centre = 1.0 - lat_coef - lat_prev - lon_coef - lon_prev
    last = jnp.where(jnp.logical_and(row == 7, at_north), 0.0, lat_coef[size - 16 : size - 8])
    lat_next = jnp.concatenate([lat_coef[: size - 16], last, lat_coef[size - 8 :]], axis=0)
    return centre, lat_next, lat_prev, lon_coef, lon_prev


def diffuse_step(h, coefs):
    size, width = h.shape
    centre, lat_coef, lat_prev, lon_coef, lon_prev = coefs
    return (
        centre * h
        + lat_coef * pltpu.roll(h, size - 1, 0)
        + lat_prev * pltpu.roll(h, 1, 0)
        + lon_coef * pltpu.roll(h, width - 1, 1)
        + lon_prev * pltpu.roll(h, 1, 1)
    )


def diffuse(fields, coefs):
    for _ in range(DSTEPS):
        fields = [[diffuse_step(h, c) for h in tiles] for tiles, c in zip(fields, coefs)]
    return fields


def main_kernel(
    place_ref, field_ref, north_ref, south_ref, lat_ref, lon_ref, cnorth_ref, csouth_ref, out_ref,
    rim_ref, crim_ref,
):
    fill_rim(rim_ref, north_ref, south_ref)
    fill_rim(crim_ref, cnorth_ref, csouth_ref)
    slabs, rows, _ = lat_ref.shape
    at_south, at_north = place_ref[0] == 1, place_ref[1] == 1

    def body(step, _):
        tiles = [4 * step + i for i in range(4)]
        coefs = [
            coefs_of(
                with_rim(lat_ref[j], crim_ref[j]),
                with_rim(lon_ref[j], crim_ref[slabs + j]),
                at_south,
                at_north,
            )
            for j in tiles
        ]
        fields = [
            [with_rim(field_ref[i], rim_ref[i]) for i in (j, slabs + j)]
            for j in tiles
        ]
        for j, results in zip(tiles, diffuse(fields, coefs)):
            for m in range(2):
                out_ref[m * slabs + j] = results[m][:rows]
        return 0

    lax.fori_loop(0, slabs // 4, body, 0)


def gather_kernel(
    place_ref, flag_ref, strip_ref, cstrip_ref, east_ref, west_ref,
    main_ref, sigma_ref, slot_ref, back_ref, grid_ref, rows_ref, back_scr,
):
    slabs, rows, columns = sigma_ref.shape
    cap = slot_ref.shape[1]
    groups = slabs // 4
    at_south, at_north = place_ref[0] == 1, place_ref[1] == 1
    size = strip_ref.shape[1]
    place = iota((size, 128), 1) % SLOT
    column = iota((rows, columns), 1)
    inner = jnp.logical_and(column >= RIM, column < columns - RIM)

    def joined(strip, east, west, g):
        east = pltpu.roll(east, (8 - RIM * g) % 128, 1)
        west = pltpu.roll(west, (12 - RIM * g) % 128, 1)
        return jnp.where(place // RIM == 2, east, jnp.where(place // RIM == 3, west, strip))

    for first in range(0, groups, 4):
        tiles = range(first, first + 4)
        coefs = [
            coefs_of(
                *(
                    joined(cstrip_ref[groups * a + g], east_ref[2 + a], west_ref[2 + a], g)
                    for a in range(2)
                ),
                at_south,
                at_north,
            )
            for g in tiles
        ]
        fields = [
            [joined(strip_ref[groups * m + g], east_ref[m], west_ref[m], g) for m in range(2)]
            for g in tiles
        ]
        for g, results in zip(tiles, diffuse(fields, coefs)):
            for m in range(2):
                h = results[m][:rows]
                outer = jnp.where(place[:rows] < 8, h, pltpu.roll(h, 120, 1))
                for i in range(4):
                    j = 4 * g + i
                    edges = pltpu.roll(outer, (120 - SLOT * i) % 128, 1)
                    whole = jnp.where(inner, main_ref[m * slabs + j], edges) * sigma_ref[j]
                    grid_ref[rows * j : rows * (j + 1), columns * m : columns * (m + 1)] = whole.astype(BF16)
    grid = grid_ref[...].T
    back_scr[...] = jnp.zeros_like(back_scr)

    def body(step, _):
        k = step * RANKS_AT_ONCE
        used = halves(flag_ref, k)
        for test, first, length in branches(used, slabs):

            @pl.when(test)
            def _():
                fill_rows(rows_ref, slot_ref, k, first, length, rows)
                part_of_grid = grid[:, rows * first : rows * (first + length)]
                picked = dot(part_of_grid, rows_ref[: rows * length])
                for i in range(RANKS_AT_ONCE):
                    weight = column_weights(slot_ref, k + i, columns)
                    for m in range(2):
                        part = picked[columns * m : columns * (m + 1), 128 * i : 128 * (i + 1)]
                        at = pl.ds(cap * m + k + i, 1)
                        back_scr[at, :] = jnp.sum(part * weight, axis=0, keepdims=True)

        return 0

    lax.fori_loop(0, cap // RANKS_AT_ONCE, body, 0)
    back_ref[...] = back_scr[...].T.astype(BF16)


def unpack_kernel(
    place_ref, back_ref, recv_ref, dest_ref, rank_ref, p_ref, r_ref, var_ref, panel_ref,
    applied_ref, sums_ref,
):
    peers = back_ref.shape[0]
    cap = back_ref.shape[1] // 2
    count = p_ref.shape[1]
    lat_count = panel_ref.shape[1] // cap
    lon_count = peers // lat_count
    recv = recv_ref[...].astype(F32)[:, 3, :].astype(BF16)
    mine = iota((16, peers), 1) == iota((16, peers), 0) * lon_count + place_ref[2]
    group = dot(mine.astype(F32).astype(BF16), recv)
    corr = jnp.zeros((2, cap), F32)
    for i in range(lat_count):
        pair = jnp.concatenate([group[i : i + 1, :cap], group[i : i + 1, cap:]], axis=0)
        corr = corr + dot(pair.astype(BF16), panel_ref[:, cap * i : cap * (i + 1)], NT)
    corr = jnp.concatenate([corr, jnp.zeros((2, BLOCK - cap), F32)], axis=1)
    back = back_ref[...].astype(F32).T.astype(BF16)
    sums = [jnp.zeros((2, BLOCK), F32) for _ in range(4)]
    for start in range(0, count, BLOCK):
        at = slice(start, start + BLOCK)
        hot = (iota((peers, BLOCK), 0) == dest_ref[:, at]).astype(F32).astype(BF16)
        rank_hot = (iota((cap, BLOCK), 0) == rank_ref[:, at].astype(jnp.int32)).astype(F32)
        values = dot(back, hot)
        forward = [
            jnp.sum(values[cap * m : cap * (m + 1)] * rank_hot, axis=0, keepdims=True)
            for m in range(2)
        ]
        p = p_ref[:, at]
        r = r_ref[:, at]
        applied = jnp.concatenate(forward, axis=0) + var_ref[:, at] * p
        if start == 0:
            applied = applied + corr
        applied_ref[:, at] = applied
        for i, product in enumerate((p * applied, r * r, r * applied, applied * applied)):
            sums[i] = sums[i] + product
    lane = iota((2, 128), 1)
    row = iota((2, 128), 0)
    out = jnp.zeros((2, 128), F32)
    for i in range(4):
        total = jnp.sum(sums[i], axis=1, keepdims=True)
        out = out + jnp.where(lane == 2 * i + row, total, 0.0)
    sums_ref[...] = jnp.broadcast_to(jnp.sum(out, axis=0, keepdims=True), (peers, 128))


def update_kernel(sums_ref, applied_ref, w_ref, r_ref, p_ref, w_out, r_out, p_out):
    sums = jnp.sum(sums_ref[...], axis=0, keepdims=True)
    for m in range(2):
        at = slice(m, m + 1)
        curvature, norm_old, cross, square = (
            sums[:, 2 * i + m : 2 * i + m + 1] for i in range(4)
        )
        step = norm_old / curvature
        norm_new = norm_old - 2.0 * step * cross + step * step * square
        p = p_ref[at]
        r_next = r_ref[at] - step * applied_ref[at]
        w_out[at] = w_ref[at] + step * p
        r_out[at] = r_next
        p_out[at] = r_next + (norm_new / norm_old) * p


def shift(value, axis, steps):
    count = lax.axis_size(axis)
    return lax.ppermute(value, axis, [(i, (i + steps) % count) for i in range(count)])


def exchange(array):
    return lax.all_to_all(array, ("lat", "lon"), split_axis=0, concat_axis=0, tiled=True)


def local(
    w_obs, r_obs, p_obs, obs_dest, obs_row, obs_col, obs_level, obs_field, obs_frac, obs_var,
    corr_panel, sigma_b, coef_lat, coef_lon,
):
    lat_count = lax.axis_size("lat")
    lon_count = lax.axis_size("lon")
    peers = lat_count * lon_count
    count = p_obs.shape[1]
    cap = 2 * count // peers
    fields, levels, rows, columns = sigma_b.shape
    slabs = fields * levels
    shape = jax.ShapeDtypeStruct
    place = jnp.stack(
        [
            (lax.axis_index("lat") == 0).astype(jnp.int32),
            (lax.axis_index("lat") == lat_count - 1).astype(jnp.int32),
            lax.axis_index("lon"),
        ]
    ).astype(jnp.int32)
    smem = pl.BlockSpec(memory_space=pltpu.SMEM)
    vmem = pl.BlockSpec(memory_space=pltpu.VMEM)
    hbm = pl.BlockSpec(memory_space=pltpu.HBM)

    sigma = sigma_b.reshape(slabs, rows, columns)
    lat_coef = coef_lat.reshape(slabs, rows, columns)
    lon_coef = coef_lon.reshape(slabs, rows, columns)
    edges = lambda at: jnp.concatenate([lat_coef[:, at], lon_coef[:, at]], axis=0).astype(BF16)
    rim = pltpu.VMEM((2 * slabs, RIM, columns), F32)
    both_rims = pltpu.VMEM((2 * slabs, 2 * RIM, columns), F32)
    coef_south = shift(edges(slice(rows - RIM, None)), "lat", 1)
    coef_north = shift(edges(slice(0, RIM)), "lat", -1)
    ext = rows + 2 * RIM
    groups = slabs // 4

    def strips(sources, *arrays):
        outer = shape((len(arrays) - sources, ext, 128), F32)
        return call(
            functools.partial(strip_kernel, sources),
            (shape((2 * groups, ext, 128), F32), outer, outer),
            24, 500_000_000, 4_000_000,
            (both_rims,),
        )(*arrays)

    cstrip, c_east, c_west = strips(2, lat_coef, lon_coef, coef_north, coef_south)

    line = lambda a: a.reshape(1, count)
    dest = line(obs_dest)
    pair = pltpu.VMEM((2, count), F32)
    single = pltpu.VMEM((1, count), jnp.int32)
    send, rank = pl.pallas_call(
        functools.partial(pack_kernel, slabs // 2, levels, rows, columns, cap),
        out_shape=(shape((peers, 4, 128), BF16), shape((1, count), F32)),
        in_specs=[hbm] * 7,
        out_specs=(vmem, vmem),
        scratch_shapes=[pair, pair] + [single] * 5 + [pltpu.SemaphoreType.DMA((7,))],
        compiler_params=pltpu.CompilerParams(vmem_limit_bytes=56 * MIB),
        cost_estimate=pl.CostEstimate(flops=2_000_000_000, bytes_accessed=500_000, transcendentals=0),
    )(p_obs, obs_frac, dest, line(obs_row), line(obs_col), line(obs_level), line(obs_field))
    recv = exchange(send)

    width = 128 * RANKS_AT_ONCE
    field, to_north, to_south, slot, flags = call(
        scatter_kernel,
        (
            shape((2 * slabs, rows, columns), F32),
            shape((2 * slabs, RIM, columns), BF16),
            shape((2 * slabs, RIM, columns), BF16),
            shape((7, cap, peers), F32),
            shape((1, 128), jnp.int32),
        ),
        32, 9_000_000_000, 4_000_000,
        (
            pltpu.VMEM((slabs * rows, width), BF16),
            pltpu.VMEM((2 * columns, width), BF16),
            pltpu.VMEM((slabs * rows, 2 * columns), F32),
            pltpu.SMEM((1, 128), jnp.int32),
            rim,
            rim,
            pltpu.SemaphoreType.DMA,
        ),
    )(recv, sigma)
    south = shift(to_north, "lat", 1)
    north = shift(to_south, "lat", -1)
    strip, to_east, to_west = strips(1, field, north, south, c_east, c_west)
    west = shift(to_east, "lon", 1)
    east = shift(to_west, "lon", -1)

    done = pl.pallas_call(
        main_kernel,
        out_shape=shape((2 * slabs, rows, columns), F32),
        in_specs=[smem] + [vmem] * 7,
        out_specs=vmem,
        scratch_shapes=[both_rims] * 2,
        compiler_params=pltpu.CompilerParams(vmem_limit_bytes=24 * MIB),
        cost_estimate=pl.CostEstimate(flops=5_000_000_000, bytes_accessed=8_000_000, transcendentals=0),
    )(place, field, north, south, lat_coef, lon_coef, coef_north, coef_south)

    back = pl.pallas_call(
        gather_kernel,
        out_shape=shape((peers, 2 * cap), BF16),
        in_specs=[smem, smem] + [vmem] * 7,
        out_specs=vmem,
        scratch_shapes=[
            pltpu.VMEM((slabs * rows, 2 * columns), BF16),
            pltpu.VMEM((slabs * rows, width), BF16),
            pltpu.VMEM((2 * cap, peers), F32),
        ],
        compiler_params=pltpu.CompilerParams(vmem_limit_bytes=36 * MIB),
        cost_estimate=pl.CostEstimate(flops=9_000_000_000, bytes_accessed=8_000_000, transcendentals=0),
    )(place, flags, strip, cstrip, east, west, done, sigma, slot)
    back = exchange(back)

    applied, sums = pl.pallas_call(
        unpack_kernel,
        out_shape=(shape((2, count), F32), shape((peers, 128), F32)),
        in_specs=[smem] + [vmem] * 8,
        out_specs=(vmem, vmem),
        compiler_params=pltpu.CompilerParams(vmem_limit_bytes=16 * MIB),
        cost_estimate=pl.CostEstimate(flops=300_000_000, bytes_accessed=500_000, transcendentals=0),
    )(place, back, recv, dest, rank, p_obs, r_obs, line(obs_var), corr_panel[0].T)
    sums = exchange(sums)
    whole = shape((2, count), F32)
    return call(update_kernel, (whole, whole, whole), 8, 100_000, 300_000)(
        sums, applied, w_obs, r_obs, p_obs
    )


def solution(mesh):
    both = ("lat", "lon")
    row = P(None, both)
    grid = P(None, None, "lat", "lon")
    in_specs = (
        row, row, row, P(both, None), P(both), P(both), P(both), P(both), row, P(both),
        P("lon", None, "lat"), grid, grid, grid,
    )
    return jax.shard_map(local, mesh=mesh, in_specs=in_specs, out_specs=(row, row, row), check_vma=False)
```
